32 devices in a mesh: elem: 8 (over y, x, core), mode: 4 (over z).
Axes of the slice: x: 2, y: 2, z: 4, core: 2. Of those that a mesh axis runs over, the one named last changes fastest.
Arguments:
- u_spec: bfloat16 [1024, 16384], P('mode', 'elem'), may hold values from -6 to 6
- dir_spec: bfloat16 [1024, 16384], P('mode', 'elem'), may hold values from -6 to 6
- advecting: bfloat16 [3, 1024, 16384], P(None, None, ('elem', 'mode')), may hold values from -6 to 6
- viscosity: bfloat16 [1024, 16384], P(None, ('elem', 'mode')), may hold values from 0.099609375 to 2
- degrees: int32 [2, 256], P(None, 'elem'), may hold values from 2 to 7
- edge_side: int32 [1024], P('elem'), may hold values from 0 to 127, as said below
- edge_link: int32 [3, 1024], P(None, 'elem'), may hold values from -1 to 127, as said below
Outputs:
- advect: float32 [1024, 16384], P('mode', 'elem')
- helm_velocity: float32 [1024, 16384], P('mode', 'elem')
- helm_direction: float32 [1024, 16384], P('mode', 'elem')
The draws below stay inside these ranges and needn't reach their ends.
Inputs may be any that keep to these rules, and one draw needn't show every extreme that they name: `edge_side`: within each partition's 128 slots, no element side appears twice. `edge_link`: A slot with peer -1 is empty and has flag 0 and peer slot 0. Pairing is symmetric: a live slot's partner is live, names it back and has the same flag. A peer is the partition itself (another slot) or a partition one or two places away around the closed loop of 8 partitions. At most 24 live slots of one partition name any one other partition as peer, and some partition has exactly that many with each of its four neighbours. Some partition has all 128 slots live.
All inputs are finite; a program needn't handle non-finite values.
Results may differ from the reference program's by a relative error of at most 0.0055.
Values may be sent and summed in bfloat16 or wider, within the bound.
No kernel may reach another device: no remote copies, remote signals or barrier semaphores. Data moves between devices by JAX's collectives and lax.ppermute only.
A program may use at most 128 MiB of HBM per device.

```python
import math
import jax
import jax.numpy as jnp
import numpy as np
from jax import lax

Q = 64
NZ = 1024
E_DEV = 32
SLOTS = 128
PARTS_SIZE = 8
E = 256
ELB = 8


def shuffled_rows(key, row_count, length):
    key_list = jax.random.split(key, row_count)

    def one_row(row_key):
        return jax.random.permutation(row_key, length).astype(jnp.int32)
    return jax.vmap(one_row)(key_list)


def edge_tables(key):
    base_key = jax.random.fold_in(key, 811)
    key_list = jax.random.split(base_key, 10)
    inner_most = SLOTS // 8
    near_most = 3 * SLOTS // 16
    parts_range = jnp.arange(PARTS_SIZE, dtype=jnp.int32)
    busy_part = jax.random.randint(key_list[0], (), 0, PARTS_SIZE)
    inner_pairs = jax.random.randint(key_list[1], (PARTS_SIZE,), 2, inner_most + 1)
    first_pairs = jax.random.randint(key_list[2], (PARTS_SIZE,), 4, near_most + 1)
    second_pairs = jax.random.randint(key_list[3], (PARTS_SIZE,), 4, near_most + 1)
    inner_pairs = jnp.where(parts_range == busy_part, inner_most, inner_pairs)
    first_pairs = jnp.where((parts_range == busy_part) | (parts_range == (busy_part + PARTS_SIZE - 1) % PARTS_SIZE), near_most, first_pairs)
    second_pairs = jnp.where((parts_range == busy_part) | (parts_range == (busy_part + PARTS_SIZE - 2) % PARTS_SIZE), near_most, second_pairs)
    inner_flip = jax.random.randint(key_list[4], (PARTS_SIZE, inner_most), 0, 2)
    first_flip = jax.random.randint(key_list[5], (PARTS_SIZE, near_most), 0, 2)
    second_flip = jax.random.randint(key_list[6], (PARTS_SIZE, near_most), 0, 2)
    owner_part = parts_range[:, None]
    place = jnp.arange(SLOTS, dtype=jnp.int32)[None, :]
    edge_a = 2 * inner_most
    edge_b = edge_a + near_most
    edge_c = edge_b + near_most
    edge_d = edge_c + near_most
    category = (place >= edge_a).astype(jnp.int32) + (place >= edge_b).astype(jnp.int32) + (place >= edge_c).astype(jnp.int32) + (place >= edge_d).astype(jnp.int32)
    category = jnp.broadcast_to(category, (PARTS_SIZE, SLOTS))
    place_full = jnp.broadcast_to(place, (PARTS_SIZE, SLOTS))
    start_of = jnp.where(category == 0, 0, edge_a + (category - 1) * near_most)
    within = place_full - start_of
    pair_index = jnp.where(category == 0, within // 2, within)
    shift_of = jnp.where(category == 0, 0, jnp.where(category == 1, 1, jnp.where(category == 2, -1, jnp.where(category == 3, 2, -2))))
    peer_index = (owner_part + shift_of + PARTS_SIZE) % PARTS_SIZE
    partner_place = jnp.where(category == 0, jnp.bitwise_xor(place_full, 1), jnp.where(category == 1, edge_b + within, jnp.where(category == 2, edge_a + within, jnp.where(category == 3, edge_d + within, edge_c + within))))
    pair_limit = jnp.where(category == 0, inner_pairs[:, None], jnp.where(category == 1, first_pairs[:, None], jnp.where(category == 2, jnp.roll(first_pairs, 1)[:, None], jnp.where(category == 3, second_pairs[:, None], jnp.roll(second_pairs, 2)[:, None]))))
    live_slot = pair_index < pair_limit
    inner_pick = jnp.take_along_axis(inner_flip, jnp.clip(pair_index, 0, inner_most - 1), axis=1)
    near_index = jnp.clip(pair_index, 0, near_most - 1)
    first_pick = jnp.take_along_axis(first_flip, near_index, axis=1)
    first_back = jnp.take_along_axis(jnp.roll(first_flip, 1, axis=0), near_index, axis=1)
    second_pick = jnp.take_along_axis(second_flip, near_index, axis=1)
    second_back = jnp.take_along_axis(jnp.roll(second_flip, 2, axis=0), near_index, axis=1)
    flip_flag = jnp.where(category == 0, inner_pick, jnp.where(category == 1, first_pick, jnp.where(category == 2, first_back, jnp.where(category == 3, second_pick, second_back))))
    slot_of = shuffled_rows(key_list[7], PARTS_SIZE, SLOTS)
    partner_slot = slot_of[peer_index, partner_place]
    inverse = jnp.argsort(slot_of, axis=1)

    def place_slots(values):
        return jnp.take_along_axis(values, inverse, axis=1)
    flip_row = place_slots(jnp.where(live_slot, flip_flag, 0))
    peer_row = place_slots(jnp.where(live_slot, peer_index, -1))
    slot_row = place_slots(jnp.where(live_slot, partner_slot, 0))
    link = jnp.stack([flip_row, peer_row, slot_row], axis=0).reshape(3, PARTS_SIZE * SLOTS).astype(jnp.int32)
    top_value = 4 * E_DEV - 1
    side_order = shuffled_rows(key_list[8], PARTS_SIZE, 4 * E_DEV)
    chosen = jax.random.randint(key_list[9], (PARTS_SIZE,), 0, SLOTS)
    where_top = jnp.argmax((side_order == top_value).astype(jnp.int32), axis=1)
    value_at = jnp.take_along_axis(side_order, chosen[:, None], axis=1)[:, 0]
    row_index = jnp.arange(PARTS_SIZE, dtype=jnp.int32)
    side_order = side_order.at[row_index, where_top].set(value_at)
    side_order = side_order.at[row_index, chosen].set(top_value)
    sides = side_order[:, :SLOTS].reshape(PARTS_SIZE * SLOTS).astype(jnp.int32)
    return (sides, link)


def draw_edge_side(key, part):
    return edge_tables(key)[0]


def draw_edge_link(key, part):
    return edge_tables(key)[1]


def with_ends(drawn, rng, least, high):
    spot = [jax.random.randint(jax.random.fold_in(rng, axis), (), 0, length) for axis, length in enumerate(drawn.shape)]
    longest = drawn.shape.index(max(drawn.shape))
    beside = spot[:longest] + [(spot[longest] + 1) % drawn.shape[longest]] + spot[longest + 1:]
    return drawn.at[tuple(spot)].set(least).at[tuple(beside)].set(high)


def steps_of(key, extent, cuts, smallest, high):
    def one(dim, shards_of):
        draws = jax.random.uniform(jax.random.fold_in(jax.random.fold_in(key, 6), dim), (shards_of,), jnp.float32, smallest / len(cuts), high / len(cuts))
        return jnp.repeat(jnp.exp(draws), extent[dim] // shards_of).reshape((-1,) + (1,) * (len(extent) - dim - 1))

    gain = one(*cuts[0])
    for cut in cuts[1:]:
        gain = gain * one(*cut)
    return gain


def centred(key, extent, spread, limit, pieces=(), kind=jnp.bfloat16):
    drawn = spread * jax.random.normal(key, extent, jnp.float32)
    if pieces:
        drawn = drawn * steps_of(key, extent, pieces, -0.22, 0.18)
    return jnp.clip(drawn, -limit, limit).astype(kind)


def setup_inputs(seed: int = 0) -> dict:
    keys = jax.random.split(jax.random.key(seed), 8)
    u_spec = centred(keys[0], (NZ, E * Q), 1.0, 6.0, ((0, 4), (1, 8)))
    dir_spec = centred(keys[1], (NZ, E * Q), 1.0, 6.0, ((0, 4), (1, 8)))
    advecting = centred(keys[2], (3, NZ, E * Q), 1.0, 6.0, ((2, 32),))
    viscosity = jnp.clip(jnp.exp(math.log(2.0) - 2.9996462 * jax.random.uniform(keys[3], (NZ, E * Q), jnp.float32) ** steps_of(keys[3], (NZ, E * Q), ((1, 32),), -0.2, 0.2)), 0.099609375, 2.0).astype(jnp.bfloat16)
    degrees = with_ends(jax.random.randint(keys[4], (2, E), 2, 8), jax.random.fold_in(keys[4], 1), 2, 7).astype(jnp.int32)
    edge_side = draw_edge_side(jax.random.fold_in(keys[7], 71), 0)
    edge_link = draw_edge_link(jax.random.fold_in(keys[7], 71), 0)
    return {"u_spec": u_spec, "dir_spec": dir_spec, "advecting": advecting, "viscosity": viscosity, "degrees": degrees, "edge_side": edge_side, "edge_link": edge_link}


METRIC = 0.125
AREA_SCALE = 64.0
LENGTH = 8.0
HELM_LAMBDA = 4.0
PENALTY = 0.02

def cheb_tables():
    degree_top = 7
    angles = np.pi * np.arange(degree_top + 1) / degree_top
    cheb_points = np.cos(angles)
    signs_scale = np.ones(degree_top + 1)
    signs_scale[0] = 2.0
    signs_scale[degree_top] = 2.0
    signs_scale = signs_scale * (-1.0) ** np.arange(degree_top + 1)
    differences = cheb_points[:, None] - cheb_points[None, :]
    derivative = signs_scale[:, None] / signs_scale[None, :] / (differences + np.eye(degree_top + 1))
    derivative = derivative - np.eye(degree_top + 1) * derivative.sum(axis=1)[:, None]
    weights = np.zeros(degree_top + 1)
    interior = np.ones(degree_top - 1)
    for k in range(1, (degree_top - 1) // 2 + 1):
        interior = interior - 2.0 * np.cos(2 * k * angles[1:degree_top]) / (4 * k * k - 1)
    weights[0] = 1.0 / (degree_top * degree_top)
    weights[degree_top] = weights[0]
    weights[1:degree_top] = 2.0 * interior / degree_top
    return (derivative, weights)

def node_tables():
    derivative, weights = cheb_tables()
    identity_eight = np.eye(8)
    node_x = np.kron(METRIC * derivative, identity_eight)
    node_y = np.kron(identity_eight, METRIC * derivative)
    mass = AREA_SCALE * np.outer(weights, weights).reshape(-1)
    edge_weight = LENGTH * weights
    return (jnp.asarray(node_x, dtype=jnp.float32), jnp.asarray(node_y, dtype=jnp.float32), jnp.asarray(mass, dtype=jnp.float32), jnp.asarray(edge_weight, dtype=jnp.float32))

def synthesis_table(total_count):
    planes = jnp.arange(total_count, dtype=jnp.int32)
    wave_index = planes // 2
    turn_count = planes[:, None] * wave_index[None, :] % total_count
    angles = 2.0 * math.pi / total_count * turn_count.astype(jnp.float32)
    level_scale = math.sqrt(2.0 / total_count)
    parity = (planes % 2)[None, :]
    synthesis = jnp.where(parity == 0, jnp.cos(angles), jnp.sin(angles)) * level_scale
    alternating = (1 - 2 * (planes % 2)).astype(jnp.float32)[:, None] / math.sqrt(total_count)
    column = planes[None, :]
    synthesis = jnp.where(column == 0, jnp.float32(1.0 / math.sqrt(total_count)), synthesis)
    synthesis = jnp.where(column == 1, alternating, synthesis)
    return synthesis.astype(jnp.bfloat16)

def z_derivative(coeffs):
    total_count = coeffs.shape[-2]
    paired = coeffs.reshape(coeffs.shape[:-2] + (total_count // 2, 2, coeffs.shape[-1]))
    rate_table = (4.0 / total_count * jnp.arange(total_count // 2, dtype=jnp.float32))[:, None]
    even_part = rate_table * paired[..., 1, :]
    odd_part = -rate_table * paired[..., 0, :]
    return jnp.stack([even_part, odd_part], axis=-2).reshape(coeffs.shape)

def side_nodes(side_code, position):
    return jnp.where(side_code == 0, position, jnp.where(side_code == 1, 8 * position + 7, jnp.where(side_code == 2, 63 - position, 8 * (7 - position))))

def reference(u_spec, dir_spec, advecting, viscosity, degrees, edge_side, edge_link):
    node_x, node_y, mass, edge_weight = node_tables()
    synthesis = synthesis_table(NZ)
    block_width = Q * ELB
    columns = jnp.arange(E * Q, dtype=jnp.int32)
    mass_columns = mass[columns % block_width // ELB]
    velocity = advecting.astype(jnp.float32)
    weighted = mass_columns[None, :] * viscosity.astype(jnp.float32)

    def node_apply(field_data, matrix):
        shaped = field_data.reshape(NZ, E // ELB, Q, ELB)
        result = jnp.einsum('pq,zbql->zbpl', matrix, shaped, precision=lax.Precision.HIGHEST)
        return result.reshape(NZ, E * Q)

    def gradients(spec_field):
        slope_hat = z_derivative(spec_field.astype(jnp.float32)).astype(jnp.bfloat16)
        plain_phys = jnp.dot(synthesis, spec_field, preferred_element_type=jnp.float32)
        along_z = jnp.dot(synthesis, slope_hat, preferred_element_type=jnp.float32)
        return (node_apply(plain_phys, node_x), node_apply(plain_phys, node_y), along_z)

    def volume(gradient_set):
        grad_x, grad_y, along_z = gradient_set
        flat_sum = node_apply(weighted * grad_x, node_x.T) + node_apply(weighted * grad_y, node_y.T)
        co_flat = jnp.dot(synthesis.T, flat_sum.astype(jnp.bfloat16), preferred_element_type=jnp.float32)
        co_span = jnp.dot(synthesis.T, (weighted * along_z).astype(jnp.bfloat16), preferred_element_type=jnp.float32)
        return co_flat - z_derivative(co_span)
    flip_flag = edge_link[0]
    peer_part = edge_link[1]
    peer_slot = edge_link[2]
    slots_all = PARTS_SIZE * SLOTS
    owner_part = jnp.arange(slots_all, dtype=jnp.int32) // SLOTS
    element = owner_part * E_DEV + edge_side // 4
    side_code = edge_side % 4
    position = jnp.arange(8, dtype=jnp.int32)
    side_node = side_nodes(side_code[:, None], position[None, :])
    slot_columns = ((element // ELB)[:, None] * block_width + side_node * ELB + (element % ELB)[:, None]).reshape(-1)
    live_slot = peer_part >= 0
    safe_peer = jnp.maximum(peer_part, 0)
    source = safe_peer * SLOTS + peer_slot
    turned = jnp.where(flip_flag[:, None] == 1, 7 - position[None, :], position[None, :])
    partner = (source[:, None] * 8 + turned).reshape(-1)
    normal_degree = jnp.where(side_code % 2 == 0, degrees[0][element], degrees[1][element]).astype(jnp.float32)
    joint_degree = jnp.maximum(normal_degree, normal_degree[source])
    strength = jnp.where(live_slot, PENALTY * (joint_degree + 1.0) * (joint_degree + 1.0), jnp.float32(0.0))
    factor = (strength[:, None] * edge_weight[None, :]).reshape(-1)

    def penalty(spec_field):
        traces = spec_field[:, slot_columns].astype(jnp.float32)
        others = traces[:, partner]
        penalty_terms = factor[None, :] * (traces - others)
        return jnp.zeros((NZ, E * Q), jnp.float32).at[:, slot_columns].add(penalty_terms)
    grads_velocity = gradients(u_spec)
    moved_phys = (velocity[0] * grads_velocity[0] + velocity[1] * grads_velocity[1] + velocity[2] * grads_velocity[2]).astype(jnp.bfloat16)
    advect = jnp.dot(synthesis.T, moved_phys, preferred_element_type=jnp.float32)
    helm_velocity = HELM_LAMBDA * mass_columns[None, :] * u_spec.astype(jnp.float32) + volume(grads_velocity) + penalty(u_spec)
    helm_direction = HELM_LAMBDA * mass_columns[None, :] * dir_spec.astype(jnp.float32) + volume(gradients(dir_spec)) + penalty(dir_spec)
    return (advect, helm_velocity, helm_direction)
```

```python
import functools
import math

import jax
import jax.numpy as jnp
import ml_dtypes
import numpy as np
from jax import lax
from jax.experimental import pallas as pl
from jax.experimental.pallas import tpu as pltpu
from jax.sharding import PartitionSpec as P

NQ = 8
METRIC = 0.125
AREA_SCALE = 64.0
LENGTH = 8.0
HELM_LAMBDA = 4.0
PENALTY = 0.02
OFFSETS = (1, 2, -1, -2)
MSG = 256
VMEM_LIMIT = 56 * 1024 * 1024

F32 = jnp.float32
BF16 = jnp.bfloat16
VMEM = pl.BlockSpec(memory_space=pltpu.VMEM)
SMEM = pl.BlockSpec(memory_space=pltpu.SMEM)
NT = (((1,), (1,)), ((), ()))


def cheb_tables():
    degree_top = 7
    angles = np.pi * np.arange(degree_top + 1) / degree_top
    cheb_points = np.cos(angles)
    signs_scale = np.ones(degree_top + 1)
    signs_scale[0] = 2.0
    signs_scale[degree_top] = 2.0
    signs_scale = signs_scale * (-1.0) ** np.arange(degree_top + 1)
    differences = cheb_points[:, None] - cheb_points[None, :]
    derivative = (
        signs_scale[:, None] / signs_scale[None, :] / (differences + np.eye(degree_top + 1))
    )
    derivative = derivative - np.eye(degree_top + 1) * derivative.sum(axis=1)[:, None]
    weights = np.zeros(degree_top + 1)
    interior = np.ones(degree_top - 1)
    for k in range(1, (degree_top - 1) // 2 + 1):
        interior = interior - 2.0 * np.cos(2 * k * angles[1:degree_top]) / (4 * k * k - 1)
    weights[0] = 1.0 / (degree_top * degree_top)
    weights[degree_top] = weights[0]
    weights[1:degree_top] = 2.0 * interior / degree_top
    return (derivative, weights)


def split_pair(matrix):
    matrix = matrix.astype(np.float32)
    high = matrix.astype(ml_dtypes.bfloat16)
    low = (matrix - high.astype(np.float32)).astype(ml_dtypes.bfloat16)
    return np.concatenate([high, high, low], axis=0)


def synthesis_tables(total):
    planes = np.arange(total)
    turn = (planes[:, None] * (planes // 2)[None, :]) % total
    angles = np.float32(2.0 * math.pi / total) * turn.astype(np.float32)
    angles = angles.astype(np.float64)
    table = np.where(planes[None, :] % 2 == 0, np.cos(angles), np.sin(angles))
    table = table * math.sqrt(2.0 / total)
    table[:, 0] = 1.0 / math.sqrt(total)
    table[:, 1] = (1 - 2 * (planes % 2)) / math.sqrt(total)
    rounded = table.astype(np.float32).astype(ml_dtypes.bfloat16)
    exact = rounded.astype(np.float64)
    rate = 4.0 / total * (planes[::2] // 2)
    sloped = np.zeros_like(exact)
    sloped[:, 1::2] = exact[:, 0::2] * rate[None, :]
    sloped[:, 0::2] = -exact[:, 1::2] * rate[None, :]
    return rounded, sloped.astype(np.float32).astype(ml_dtypes.bfloat16)


def shift_of(number):
    assert number & (number - 1) == 0
    return number.bit_length() - 1


def dot(a, b):
    return jnp.dot(a, b, preferred_element_type=F32)


def dot_split(value, table):
    high = value.astype(BF16)
    low = (value - high.astype(F32)).astype(BF16)
    return dot(jnp.concatenate([high, low, high], axis=1), table)


def planes_kernel(
    modes, advected, me_ref, *refs
):
    pieces = refs[:modes]
    (s_ref, sz_ref, t_ref, tz_ref, visc_ref, mass_ref, rx_ref, ry_ref, kx_ref, ky_ref) = refs[
        modes : modes + 10
    ]
    refs = refs[modes + 10 :]
    if advected:
        adv_ref = refs[0]
        refs = refs[1:]
    outs = refs[:modes]
    spec, flat, flux = refs[modes : modes + 3]
    moved = refs[modes + 3] if advected else None
    me = me_ref[0]
    rows = pieces[0].shape[0]
    total, width = visc_ref.shape
    group = ry_ref.shape[1]
    for d in range(modes):
        block = lax.rem(me - d + modes, modes)
        spec[pl.ds(pl.multiple_of(block * rows, rows), rows), :] = pieces[d][...]
    chunk = min(256, total)

    def grouped(value, ref):
        parts = [
            dot_split(value[:, g : g + group], ref[...]) for g in range(0, width, group)
        ]
        return parts[0] if len(parts) == 1 else jnp.concatenate(parts, axis=1)

    def forward(step, carry):
        at = pl.ds(pl.multiple_of(step * chunk, chunk), chunk)
        coeffs = spec[...]
        plain = dot(s_ref[at, :], coeffs)
        along = dot(sz_ref[at, :], coeffs)
        grad_x = dot_split(plain, rx_ref[...])
        grad_y = grouped(plain, ry_ref)
        weighted = mass_ref[...] * visc_ref[at, :].astype(F32)
        if advected:
            moved[at, :] = (
                adv_ref[0, at, :].astype(F32) * grad_x
                + adv_ref[1, at, :].astype(F32) * grad_y
                + adv_ref[2, at, :].astype(F32) * along
            ).astype(BF16)
        flux[at, :] = (weighted * along).astype(BF16)
        flat_sum = dot_split(weighted * grad_x, kx_ref[...]) + grouped(weighted * grad_y, ky_ref)
        flat[at, :] = flat_sum.astype(BF16)
        return carry

    lax.fori_loop(0, total // chunk, forward, 0)

    for d in range(modes):
        block = lax.rem(me + d, modes)
        at = pl.ds(pl.multiple_of(block * rows, rows), rows)
        volume = dot(t_ref[at, :], flat[...]) + dot(tz_ref[at, :], flux[...])
        if advected:
            outs[d][0] = dot(t_ref[at, :], moved[...]).astype(BF16)
            outs[d][1] = volume.astype(BF16)
        else:
            outs[d][0] = volume.astype(BF16)


def planes(pieces, tables, visc, adv, me):
    modes = len(pieces)
    rows, width = pieces[0].shape
    total = visc.shape[0]
    advected = adv is not None
    fields = 2 if advected else 1
    operands = [me, *pieces, *tables[:4], visc, *tables[4:]]
    if advected:
        operands.append(adv)
    scratch = [pltpu.VMEM((total, width), BF16)] * (4 if advected else 3)
    flops = 2 * total * total * width * (2 + 2 + (1 if advected else 0))
    flops += 2 * total * width * width * 9
    return pl.pallas_call(
        functools.partial(planes_kernel, modes, advected),
        out_shape=[jax.ShapeDtypeStruct((fields, rows, width), BF16)] * modes,
        in_specs=[SMEM] + [VMEM] * (len(operands) - 1),
        out_specs=[VMEM] * modes,
        scratch_shapes=scratch,
        compiler_params=pltpu.CompilerParams(vmem_limit_bytes=VMEM_LIMIT),
        cost_estimate=pl.CostEstimate(
            flops=flops, bytes_accessed=12 * total * total, transcendentals=0
        ),
        name="planes_moved" if advected else "planes_plain",
    )(*operands)


def slot_line(side, block_elements):
    element = lax.shift_right_logical(side, 2)
    code = jnp.bitwise_and(side, 3)
    first = jnp.where(code == 0, 0, jnp.where(code == 1, 7, jnp.where(code == 2, 63, 56)))
    step = jnp.where(code == 0, 1, jnp.where(code == 1, 8, jnp.where(code == 2, -1, -8)))
    block = lax.shift_right_logical(element, shift_of(block_elements))
    inner = jnp.bitwise_and(element, block_elements - 1)
    base = block * (NQ * NQ * block_elements) + first * block_elements + inner
    return base, step * block_elements


def across(values):
    return jnp.sum(values.astype(F32), axis=1, keepdims=True)


def down(values):
    return jnp.sum(values.astype(F32), axis=0, keepdims=True)


def degree_column(side_col, degrees):
    slots = side_col.shape[0]
    elements = degrees.shape[1]
    lanes = lax.broadcasted_iota(jnp.int32, (slots, elements), 1)
    mine = lanes == lax.shift_right_logical(side_col, 2)
    along_x = jnp.bitwise_and(side_col, 1) == 0
    value = jnp.where(along_x, degrees[0:1, :], degrees[1:2, :])
    return across(jnp.where(mine, value, 0))


def traces_kernel(parts, block_elements, me_ref, u_ref, d_ref, row_ref, col_ref, deg_ref, *outs):
    me = me_ref[0]
    rows, columns = u_ref.shape
    side_col = col_ref[:, 0:1]
    peer_col = col_ref[:, 2:3]
    peer_row = row_ref[2:3, :]
    slots = side_col.shape[0]
    base, step = slot_line(side_col, block_elements)
    degree = degree_column(side_col, deg_ref[...])
    before = lax.broadcasted_iota(jnp.int32, (slots, slots), 1) < lax.broadcasted_iota(
        jnp.int32, (slots, slots), 0
    )
    lane = lax.broadcasted_iota(jnp.int32, (slots, MSG), 1)
    place = lax.shift_right_logical(lane, 3)
    line = base + step * jnp.bitwise_and(lane, 7) + 1
    chunk = min(512, columns)
    for out, offset in zip(outs, OFFSETS):
        peer = lax.rem(me + offset + parts, parts)
        rank = across(jnp.where((peer_row == peer) & before, 1, 0)).astype(jnp.int32)
        chosen = (peer_col == peer) & (rank == place)
        target = down(jnp.where(chosen, line, 0)).astype(jnp.int32) - 1
        total_u = jnp.zeros((rows, MSG), F32)
        total_d = jnp.zeros((rows, MSG), F32)
        for start in range(0, columns, chunk):
            here = lax.broadcasted_iota(jnp.int32, (chunk, MSG), 0) + start
            pick = jnp.where(here == target, 1.0, 0.0).astype(BF16)
            total_u += dot(u_ref[:, start : start + chunk], pick)
            total_d += dot(d_ref[:, start : start + chunk], pick)
        out[0:rows, :] = total_u.astype(BF16)
        out[rows : 2 * rows, :] = total_d.astype(BF16)
        degrees = down(jnp.where(chosen, degree, 0.0))
        out[2 * rows :, :] = jnp.broadcast_to(degrees, (16, MSG)).astype(BF16)


def penalty_kernel(
    parts,
    block_elements,
    me_ref,
    u_ref,
    d_ref,
    row_ref,
    col_ref,
    deg_ref,
    degt_ref,
    weight_ref,
    mass_ref,
    near0,
    near1,
    near2,
    near3,
    out_u,
    out_d,
    others,
):
    near = (near0, near1, near2, near3)
    me = me_ref[0]
    rows, columns = u_ref.shape
    side_col, flag_col, peer_col, slot_col = (col_ref[:, i : i + 1] for i in range(4))
    side_row, peer_row, slot_row = row_ref[0:1, :], row_ref[2:3, :], row_ref[3:4, :]
    slots = side_col.shape[0]
    nodes = slots * NQ
    base_col, step_col = slot_line(side_col, block_elements)
    base_row, step_row = slot_line(side_row, block_elements)
    degree_col = degree_column(side_col, deg_ref[...])
    elements = degt_ref.shape[0]
    level = lax.broadcasted_iota(jnp.int32, (elements, slots), 0)
    mine = level == lax.shift_right_logical(side_row, 2)
    value = jnp.where(jnp.bitwise_and(side_row, 1) == 0, degt_ref[:, 0:1], degt_ref[:, 1:2])
    degree_row = down(jnp.where(mine, value, 0))

    lane_slot = lax.broadcasted_iota(jnp.int32, (slots, slots), 1)
    partner = lane_slot == slot_col
    partner_base = across(jnp.where(partner, base_row, 0)).astype(jnp.int32)
    partner_step = across(jnp.where(partner, step_row, 0)).astype(jnp.int32)
    inner_degree = across(jnp.where(partner, degree_row, 0.0))
    rank = across(jnp.where((peer_row == peer_col) & (slot_row < slot_col), 1, 0)).astype(
        jnp.int32
    )
    source = partner_base
    source_step = partner_step
    other_degree = inner_degree
    lane_msg = lax.broadcasted_iota(jnp.int32, (slots, MSG), 1)
    at_rank = lane_msg == rank * NQ
    for index, offset in enumerate(OFFSETS):
        from_here = peer_col == lax.rem(me + offset + parts, parts)
        far_degree = near[index][2 * rows : 2 * rows + 16, :].astype(F32)[0:1, :]
        source = jnp.where(from_here, columns + index * MSG + rank * NQ, source)
        source_step = jnp.where(from_here, 1, source_step)
        other_degree = jnp.where(
            from_here, across(jnp.where(at_rank, far_degree, 0.0)), other_degree
        )
    live = peer_col >= 0
    turned = flag_col == 1
    source = jnp.where(turned, source + 7 * source_step, source)
    source_step = jnp.where(turned, -source_step, source_step)
    source = jnp.where(live, source, -1)
    source_step = jnp.where(live, source_step, 0)
    joint = jnp.maximum(degree_col, other_degree) + 1.0
    strength = jnp.where(live, PENALTY * joint * joint, 0.0)

    lane = lax.broadcasted_iota(jnp.int32, (slots, nodes), 1)
    owner = lax.shift_right_logical(lane, 3) == lax.broadcasted_iota(jnp.int32, (slots, nodes), 0)
    node = jnp.bitwise_and(lane, 7)
    own_line = down(jnp.where(owner, base_col + step_col * node, 0)).astype(jnp.int32)
    far_line = down(jnp.where(owner, source + source_step * node, 0)).astype(jnp.int32)
    factor = down(jnp.where(owner, strength, 0.0)) * weight_ref[...]
    factor_high = factor.astype(BF16).astype(F32)
    factor_low = factor - factor_high

    chunk = min(512, columns)
    total_u = jnp.zeros((rows, nodes), F32)
    total_d = jnp.zeros((rows, nodes), F32)
    for start in range(0, columns, chunk):
        here = lax.broadcasted_iota(jnp.int32, (chunk, nodes), 0) + start
        pick = jnp.where(here == far_line, 1.0, 0.0).astype(BF16)
        total_u += dot(u_ref[:, start : start + chunk], pick)
        total_d += dot(d_ref[:, start : start + chunk], pick)
    for index in range(len(OFFSETS)):
        here = lax.broadcasted_iota(jnp.int32, (MSG, nodes), 0) + (columns + index * MSG)
        pick = jnp.where(here == far_line, 1.0, 0.0).astype(BF16)
        total_u += dot(near[index][0:rows, :], pick)
        total_d += dot(near[index][rows : 2 * rows, :], pick)
    others[0:rows, :] = total_u.astype(BF16)
    others[rows : 2 * rows, :] = total_d.astype(BF16)
    others[2 * rows :, :] = jnp.ones((16, nodes), BF16)

    for start in range(0, columns, chunk):
        here = lax.broadcasted_iota(jnp.int32, (chunk, nodes), 0) + start
        match = here == own_line
        spread_high = jnp.where(match, factor_high, 0.0).astype(BF16)
        spread_low = jnp.where(match, factor_low, 0.0).astype(BF16)
        pulled = lax.dot_general(
            others[...], spread_high, NT, preferred_element_type=F32
        ) + lax.dot_general(others[...], spread_low, NT, preferred_element_type=F32)
        at = slice(start, start + chunk)
        scale = HELM_LAMBDA * mass_ref[:, at] + pulled[2 * rows : 2 * rows + 1, :]
        out_u[:, at] = scale * u_ref[:, at].astype(F32) - pulled[0:rows, :]
        out_d[:, at] = scale * d_ref[:, at].astype(F32) - pulled[rows : 2 * rows, :]


def finish_kernel(modes, plane, me_ref, *refs):
    pieces = refs[:modes]
    local = refs[modes] if len(refs) == modes + 2 else None
    out = refs[-1]
    me = me_ref[0]
    width = pieces[0].shape[2]
    for d in range(modes):
        block = lax.rem(me - d + modes, modes)
        at = pl.ds(pl.multiple_of(block * width, width), width)
        value = pieces[d][plane].astype(F32)
        if local is not None:
            value = value + local[:, at]
        out[:, at] = value


def finish(pieces, plane, local, me):
    modes = len(pieces)
    rows, width = pieces[0].shape[1:]
    operands = [me, *pieces] + ([] if local is None else [local])
    return pl.pallas_call(
        functools.partial(finish_kernel, modes, plane),
        out_shape=jax.ShapeDtypeStruct((rows, modes * width), F32),
        in_specs=[SMEM] + [VMEM] * (len(operands) - 1),
        out_specs=VMEM,
        compiler_params=pltpu.CompilerParams(vmem_limit_bytes=VMEM_LIMIT),
        name="finish",
    )(*operands)


def pass_kernel(*refs):
    del refs


def after(values, others):
    anywhere = pl.BlockSpec(memory_space=pl.ANY)
    return pl.pallas_call(
        pass_kernel,
        out_shape=[jax.ShapeDtypeStruct(v.shape, v.dtype) for v in values],
        in_specs=[anywhere] * (len(values) + len(others)),
        out_specs=[anywhere] * len(values),
        input_output_aliases={i: i for i in range(len(values))},
        name="after",
    )(*values, *others)


def shift_by(block, axis, distance):
    count = lax.axis_size(axis)
    return lax.ppermute(block, axis, [(i, (i + distance) % count) for i in range(count)])


def on_device(u_spec, dir_spec, advecting, viscosity, degrees, edge_side, edge_link):
    modes = lax.axis_size("mode")
    parts = lax.axis_size("elem")
    total, width = viscosity.shape
    rows, columns = u_spec.shape
    block_elements = degrees.shape[1] // modes
    slots = edge_side.shape[0]
    my_mode = lax.axis_index("mode")
    mode_id = my_mode.astype(jnp.int32).reshape(1)
    part_id = lax.axis_index("elem").astype(jnp.int32).reshape(1)

    derivative, weights = cheb_tables()
    identity = np.eye(block_elements)
    kron_x = np.kron(METRIC * derivative, np.eye(NQ * block_elements))
    group = width
    if width % 256 == 0 and 256 % (NQ * block_elements) == 0:
        group = 256
    kron_y = np.kron(np.eye(group // (NQ * block_elements)), np.kron(METRIC * derivative, identity))
    mass = np.repeat(AREA_SCALE * np.outer(weights, weights).reshape(-1), block_elements)
    synthesis, sloped = synthesis_tables(total)
    tables = [
        jnp.asarray(t)
        for t in (
            synthesis,
            sloped,
            np.ascontiguousarray(synthesis.T),
            np.ascontiguousarray(sloped.T),
            mass.astype(np.float32)[None, :],
            split_pair(kron_x.T),
            split_pair(kron_y.T),
            split_pair(kron_x),
            split_pair(kron_y),
        )
    ]

    def cut(field):
        return [
            lax.dynamic_slice_in_dim(field, lax.rem(my_mode + d, modes) * width, width, axis=1)
            for d in range(modes)
        ]

    u_cut = cut(u_spec)
    u_pieces = [u_cut[0]] + [shift_by(u_cut[d], "mode", d) for d in range(1, modes)]
    d_cut = cut(dir_spec)
    d_send = after(d_cut[1:], u_pieces[1:])
    d_pieces = [d_cut[0]] + [shift_by(d_send[d - 1], "mode", d) for d in range(1, modes)]

    table_row = jnp.concatenate([edge_side[None, :], edge_link], axis=0)
    table_col = table_row.T
    near = pl.pallas_call(
        functools.partial(traces_kernel, parts, block_elements),
        out_shape=[jax.ShapeDtypeStruct((2 * rows + 16, MSG), BF16)] * len(OFFSETS),
        in_specs=[SMEM] + [VMEM] * 5,
        out_specs=[VMEM] * len(OFFSETS),
        compiler_params=pltpu.CompilerParams(vmem_limit_bytes=VMEM_LIMIT),
        name="traces",
    )(part_id, u_spec, dir_spec, table_row, table_col, degrees)
    by_offset = {o: shift_by(block, "elem", o) for o, block in zip(OFFSETS, near)}
    near = [by_offset[-o] for o in OFFSETS]

    u_back = planes(u_pieces, tables, viscosity, advecting, mode_id)
    d_back = planes(d_pieces, tables, viscosity, None, mode_id)

    edge_weight = np.tile(LENGTH * weights, slots).astype(np.float32)[None, :]
    mass_local = np.tile(mass, modes).astype(np.float32)[None, :]
    local_u, local_d = pl.pallas_call(
        functools.partial(penalty_kernel, parts, block_elements),
        out_shape=[jax.ShapeDtypeStruct((rows, columns), F32)] * 2,
        in_specs=[SMEM] + [VMEM] * 12,
        out_specs=[VMEM] * 2,
        scratch_shapes=[pltpu.VMEM((2 * rows + 16, slots * NQ), BF16)],
        compiler_params=pltpu.CompilerParams(vmem_limit_bytes=VMEM_LIMIT),
        cost_estimate=pl.CostEstimate(
            flops=2 * 2 * rows * slots * NQ * 3 * columns,
            bytes_accessed=20 * rows * columns,
            transcendentals=0,
        ),
        name="penalty",
    )(
        part_id,
        u_spec,
        dir_spec,
        table_row,
        table_col,
        degrees,
        degrees.T,
        jnp.asarray(edge_weight),
        jnp.asarray(mass_local),
        *near,
    )

    def returned(back):
        return [back[0]] + [shift_by(back[d], "mode", d) for d in range(1, modes)]

    u_returned = returned(u_back)
    d_returned = returned(d_back)
    advect = finish(u_returned, 0, None, mode_id)
    helm_velocity = finish(u_returned, 1, local_u, mode_id)
    helm_direction = finish(d_returned, 0, local_d, mode_id)
    return (advect, helm_velocity, helm_direction)


def solution(mesh):
    in_specs = (
        P("mode", "elem"),
        P("mode", "elem"),
        P(None, None, ("elem", "mode")),
        P(None, ("elem", "mode")),
        P(None, "elem"),
        P("elem"),
        P(None, "elem"),
    )
    out_specs = (P("mode", "elem"), P("mode", "elem"), P("mode", "elem"))
    return jax.shard_map(
        on_device, mesh=mesh, in_specs=in_specs, out_specs=out_specs, check_vma=False
    )
```

```python
import functools
import math

import jax
import jax.numpy as jnp
import ml_dtypes
import numpy as np
from jax import lax
from jax.experimental import pallas as pl
from jax.experimental.pallas import tpu as pltpu
from jax.sharding import PartitionSpec as P

NQ = 8
METRIC = 0.125
AREA_SCALE = 64.0
LENGTH = 8.0
HELM_LAMBDA = 4.0
PENALTY = 0.02
OFFSETS = (1, 2, -1, -2)
MSG = 256
MIB = 1024 * 1024
PLANES_LIMIT = 56

F32 = jnp.float32
BF16 = jnp.bfloat16
VMEM = pl.BlockSpec(memory_space=pltpu.VMEM)
SMEM = pl.BlockSpec(memory_space=pltpu.SMEM)
NT = (((1,), (1,)), ((), ()))


def cheb_tables():
    degree_top = 7
    angles = np.pi * np.arange(degree_top + 1) / degree_top
    cheb_points = np.cos(angles)
    signs_scale = np.ones(degree_top + 1)
    signs_scale[0] = 2.0
    signs_scale[degree_top] = 2.0
    signs_scale = signs_scale * (-1.0) ** np.arange(degree_top + 1)
    differences = cheb_points[:, None] - cheb_points[None, :]
    derivative = (
        signs_scale[:, None] / signs_scale[None, :] / (differences + np.eye(degree_top + 1))
    )
    derivative = derivative - np.eye(degree_top + 1) * derivative.sum(axis=1)[:, None]
    weights = np.zeros(degree_top + 1)
    interior = np.ones(degree_top - 1)
    for k in range(1, (degree_top - 1) // 2 + 1):
        interior = interior - 2.0 * np.cos(2 * k * angles[1:degree_top]) / (4 * k * k - 1)
    weights[0] = 1.0 / (degree_top * degree_top)
    weights[degree_top] = weights[0]
    weights[1:degree_top] = 2.0 * interior / degree_top
    return (derivative, weights)


def split_pair(matrix):
    matrix = matrix.astype(np.float32)
    high = matrix.astype(ml_dtypes.bfloat16)
    low = (matrix - high.astype(np.float32)).astype(ml_dtypes.bfloat16)
    return np.concatenate([high, high, low], axis=0)


def synthesis_tables(total):
    planes = np.arange(total)
    turn = (planes[:, None] * (planes // 2)[None, :]) % total
    angles = np.float32(2.0 * math.pi / total) * turn.astype(np.float32)
    angles = angles.astype(np.float64)
    table = np.where(planes[None, :] % 2 == 0, np.cos(angles), np.sin(angles))
    table = table * math.sqrt(2.0 / total)
    table[:, 0] = 1.0 / math.sqrt(total)
    table[:, 1] = (1 - 2 * (planes % 2)) / math.sqrt(total)
    rounded = table.astype(np.float32).astype(ml_dtypes.bfloat16)
    exact = rounded.astype(np.float64)
    rate = 4.0 / total * (planes[::2] // 2)
    sloped = np.zeros_like(exact)
    sloped[:, 1::2] = exact[:, 0::2] * rate[None, :]
    sloped[:, 0::2] = -exact[:, 1::2] * rate[None, :]
    return rounded, sloped.astype(np.float32).astype(ml_dtypes.bfloat16)


def shift_of(number):
    assert number & (number - 1) == 0
    return number.bit_length() - 1


def dot(a, b):
    return jnp.dot(a, b, preferred_element_type=F32)


def dot_split(value, table):
    high = value.astype(BF16)
    low = (value - high.astype(F32)).astype(BF16)
    return dot(jnp.concatenate([high, low, high], axis=1), table)


def planes_kernel(modes, chunk, advected, me_ref, *refs):
    own_ref, pieces = refs[0], refs[1:modes]
    s_in, sz_in, t_in, tz_in, *node_in = refs[modes : modes + 8]
    visc_in, mass_ref = refs[modes + 8 : modes + 10]
    refs = refs[modes + 10 :]
    if advected:
        adv_in, refs = refs[0], refs[1:]
    outs = refs[:modes]
    spec, flat, flux, s_ref, sz_ref, t_ref, tz_ref, visc_ref = refs[modes : modes + 8]
    rx_ref, ry_ref, kx_ref, ky_ref = node_refs = refs[modes + 8 : modes + 12]
    held, step_sem, node_sem, own_sem, back_sem, out_sem = refs[modes + 12 : modes + 18]
    if advected:
        moved, adv_ref = refs[modes + 18 :]
    me = me_ref[0]
    rows = own_ref.shape[0]
    total, width = visc_ref.shape
    group = ry_ref.shape[1]
    steps = total // chunk

    own_copy = pltpu.make_async_copy(
        own_ref.at[:, pl.ds(pl.multiple_of(me * width, width), width)],
        spec.at[pl.ds(pl.multiple_of(me * rows, rows), rows), :],
        own_sem,
    )
    node_copies = [
        pltpu.make_async_copy(source, target, node_sem.at[i])
        for i, (source, target) in enumerate(zip(node_in, node_refs))
    ]
    back_copies = [
        pltpu.make_async_copy(t_in, t_ref, back_sem.at[0]),
        pltpu.make_async_copy(tz_in, tz_ref, back_sem.at[1]),
    ]

    def plane_copies(step):
        at = pl.ds(pl.multiple_of(step * chunk, chunk), chunk)
        pairs = [(s_in, s_ref), (sz_in, sz_ref), (visc_in, visc_ref)]
        copies = [
            pltpu.make_async_copy(source.at[at, :], target.at[at, :], step_sem.at[step, i])
            for i, (source, target) in enumerate(pairs)
        ]
        if advected:
            copies.append(
                pltpu.make_async_copy(
                    adv_in.at[:, at, :], adv_ref.at[:, at, :], step_sem.at[step, 3]
                )
            )
        return copies

    own_copy.start()
    first = plane_copies(0)
    for copy in first[:2] + node_copies[:2] + first[2:] + node_copies[2:]:
        copy.start()
    for step in range(1, steps):
        for copy in plane_copies(step):
            copy.start()
    for copy in back_copies:
        copy.start()
    for d in range(1, modes):
        at = pl.ds(pl.multiple_of(jnp.bitwise_xor(me, d) * rows, rows), rows)
        spec[at, :] = pieces[d - 1][...]
    own_copy.wait()

    def grouped(value, ref):
        parts = [
            dot_split(value[:, g : g + group], ref[...]) for g in range(0, width, group)
        ]
        return parts[0] if len(parts) == 1 else jnp.concatenate(parts, axis=1)

    def forward(step, carry):
        at = pl.ds(pl.multiple_of(step * chunk, chunk), chunk)
        copies = plane_copies(step)
        for copy in copies[:2]:
            copy.wait()
        coeffs = spec[...]
        plain = dot(s_ref[at, :], coeffs)
        along = dot(sz_ref[at, :], coeffs)

        @pl.when(step == 0)
        def _():
            for copy in node_copies:
                copy.wait()

        for copy in copies[2:]:
            copy.wait()
        grad_x = dot_split(plain, rx_ref[...])
        grad_y = grouped(plain, ry_ref)
        weighted = mass_ref[...] * visc_ref[at, :].astype(F32)
        if advected:
            moved[at, :] = (
                adv_ref[0, at, :].astype(F32) * grad_x
                + adv_ref[1, at, :].astype(F32) * grad_y
                + adv_ref[2, at, :].astype(F32) * along
            ).astype(BF16)
        flux[at, :] = (weighted * along).astype(BF16)
        flat_sum = dot_split(weighted * grad_x, kx_ref[...]) + grouped(weighted * grad_y, ky_ref)
        flat[at, :] = flat_sum.astype(BF16)
        return carry

    lax.fori_loop(0, steps, forward, 0)

    for copy in back_copies:
        copy.wait()
    stores = [pltpu.make_async_copy(held.at[d], outs[d], out_sem.at[d]) for d in range(modes)]
    for d in [*range(1, modes), 0]:
        at = pl.ds(pl.multiple_of(jnp.bitwise_xor(me, d) * rows, rows), rows)
        volume = dot(t_ref[at, :], flat[...]) + dot(tz_ref[at, :], flux[...])
        if advected:
            held[d, 0] = dot(t_ref[at, :], moved[...]).astype(BF16)
            held[d, 1] = volume.astype(BF16)
        else:
            held[d, 0] = volume.astype(BF16)
        stores[d].start()
    for store in stores:
        store.wait()


def planes(pieces, tables, visc, mass, adv, me):
    modes = len(pieces)
    rows = pieces[0].shape[0]
    total, width = visc.shape
    group = tables[5].shape[1]
    chunk = min(256, total)
    advected = adv is not None
    fields = 2 if advected else 1
    operands = [me, *pieces, *tables, visc, mass] + ([adv] if advected else [])
    flops = 2 * total * total * width * (2 + 2 + (1 if advected else 0))
    flops += 2 * total * width * width * 9
    far = pl.BlockSpec(memory_space=pltpu.HBM)
    plane = pltpu.VMEM((total, width), BF16)
    square = pltpu.VMEM((total, total), BF16)
    node_x = pltpu.VMEM((3 * width, width), BF16)
    node_y = pltpu.VMEM((3 * group, group), BF16)
    scratch = [plane] * 3 + [square] * 4 + [plane, node_x, node_y, node_x, node_y]
    scratch += [
        pltpu.VMEM((modes, fields, rows, width), BF16),
        pltpu.SemaphoreType.DMA((total // chunk, 4)),
        pltpu.SemaphoreType.DMA((4,)),
        pltpu.SemaphoreType.DMA,
        pltpu.SemaphoreType.DMA((2,)),
        pltpu.SemaphoreType.DMA((modes,)),
    ]
    if advected:
        scratch += [plane, pltpu.VMEM(adv.shape, BF16)]
    return pl.pallas_call(
        functools.partial(planes_kernel, modes, chunk, advected),
        out_shape=[jax.ShapeDtypeStruct((fields, rows, width), BF16)] * modes,
        in_specs=[SMEM, far]
        + [VMEM] * (modes - 1)
        + [far] * (len(tables) + 1)
        + [VMEM]
        + [far] * (1 if advected else 0),
        out_specs=[far] * modes,
        scratch_shapes=scratch,
        compiler_params=pltpu.CompilerParams(vmem_limit_bytes=PLANES_LIMIT * MIB),
        cost_estimate=pl.CostEstimate(
            flops=flops, bytes_accessed=12 * total * total, transcendentals=0
        ),
        name="planes_moved" if advected else "planes_plain",
    )(*operands)


def slot_line(side, block_elements):
    element = lax.shift_right_logical(side, 2)
    code = jnp.bitwise_and(side, 3)
    first = jnp.where(code == 0, 0, jnp.where(code == 1, 7, jnp.where(code == 2, 63, 56)))
    step = jnp.where(code == 0, 1, jnp.where(code == 1, 8, jnp.where(code == 2, -1, -8)))
    block = lax.shift_right_logical(element, shift_of(block_elements))
    inner = jnp.bitwise_and(element, block_elements - 1)
    base = block * (NQ * NQ * block_elements) + first * block_elements + inner
    return base, step * block_elements


def across(values):
    return jnp.sum(values.astype(F32), axis=1, keepdims=True)


def down(values):
    return jnp.sum(values.astype(F32), axis=0, keepdims=True)


def degree_column(side_col, degrees):
    slots = side_col.shape[0]
    elements = degrees.shape[1]
    lanes = lax.broadcasted_iota(jnp.int32, (slots, elements), 1)
    mine = lanes == lax.shift_right_logical(side_col, 2)
    along_x = jnp.bitwise_and(side_col, 1) == 0
    value = jnp.where(along_x, degrees[0:1, :], degrees[1:2, :])
    return across(jnp.where(mine, value, 0))


def fetch(source, target, sem):
    return pltpu.make_async_copy(source, target, sem)


def traces_kernel(parts, block_elements, me_ref, u_in, d_in, row_ref, col_ref, deg_ref, *refs):
    out, u_ref, d_ref, sem = refs
    copies = [fetch(u_in, u_ref, sem.at[0]), fetch(d_in, d_ref, sem.at[1])]
    for copy in copies:
        copy.start()
    me = me_ref[0]
    rows, columns = u_ref.shape
    side_col = col_ref[:, 0:1]
    peer_col = col_ref[:, 2:3]
    peer_row = row_ref[2:3, :]
    slots = side_col.shape[0]
    base, step = slot_line(side_col, block_elements)
    degree = degree_column(side_col, deg_ref[...])
    before = lax.broadcasted_iota(jnp.int32, (slots, slots), 1) < lax.broadcasted_iota(
        jnp.int32, (slots, slots), 0
    )
    lane = lax.broadcasted_iota(jnp.int32, (slots, MSG), 1)
    place = lax.shift_right_logical(lane, 3)
    line = base + step * jnp.bitwise_and(lane, 7) + 1
    chunk = min(512, columns)
    for copy in copies:
        copy.wait()
    for offset in OFFSETS:
        peer = lax.rem(me + offset + parts, parts)
        rank = across(jnp.where((peer_row == peer) & before, 1, 0)).astype(jnp.int32)
        chosen = (peer_col == peer) & (rank == place)
        target = down(jnp.where(chosen, line, 0)).astype(jnp.int32) - 1
        total_u = jnp.zeros((rows, MSG), F32)
        total_d = jnp.zeros((rows, MSG), F32)
        for start in range(0, columns, chunk):
            here = lax.broadcasted_iota(jnp.int32, (chunk, MSG), 0) + start
            pick = jnp.where(here == target, 1.0, 0.0).astype(BF16)
            total_u += dot(u_ref[:, start : start + chunk], pick)
            total_d += dot(d_ref[:, start : start + chunk], pick)
        out[peer, 0:rows, :] = total_u.astype(BF16)
        out[peer, rows : 2 * rows, :] = total_d.astype(BF16)
        degrees = down(jnp.where(chosen, degree, 0.0))
        out[peer, 2 * rows :, :] = jnp.broadcast_to(degrees, (16, MSG)).astype(BF16)


def penalty_kernel(
    parts,
    block_elements,
    me_ref,
    u_in,
    d_in,
    row_ref,
    col_ref,
    deg_ref,
    degt_ref,
    weight_ref,
    mass_ref,
    near_in,
    out_u,
    out_d,
    others,
    u_ref,
    d_ref,
    sem,
    near,
    near_sem,
):
    me = me_ref[0]
    near_copies = [
        fetch(near_in.at[lax.rem(me + offset + parts, parts)], near.at[i], near_sem.at[i])
        for i, offset in enumerate(OFFSETS)
    ]
    copies = [fetch(u_in, u_ref, sem.at[0]), fetch(d_in, d_ref, sem.at[1])]
    for copy in near_copies + copies:
        copy.start()
    rows, columns = u_ref.shape
    side_col, flag_col, peer_col, slot_col = (col_ref[:, i : i + 1] for i in range(4))
    side_row, peer_row, slot_row = row_ref[0:1, :], row_ref[2:3, :], row_ref[3:4, :]
    slots = side_col.shape[0]
    nodes = slots * NQ
    base_col, step_col = slot_line(side_col, block_elements)
    base_row, step_row = slot_line(side_row, block_elements)
    degree_col = degree_column(side_col, deg_ref[...])
    elements = degt_ref.shape[0]
    level = lax.broadcasted_iota(jnp.int32, (elements, slots), 0)
    mine = level == lax.shift_right_logical(side_row, 2)
    value = jnp.where(jnp.bitwise_and(side_row, 1) == 0, degt_ref[:, 0:1], degt_ref[:, 1:2])
    degree_row = down(jnp.where(mine, value, 0))

    lane_slot = lax.broadcasted_iota(jnp.int32, (slots, slots), 1)
    partner = lane_slot == slot_col
    partner_base = across(jnp.where(partner, base_row, 0)).astype(jnp.int32)
    partner_step = across(jnp.where(partner, step_row, 0)).astype(jnp.int32)
    inner_degree = across(jnp.where(partner, degree_row, 0.0))
    rank = across(jnp.where((peer_row == peer_col) & (slot_row < slot_col), 1, 0)).astype(
        jnp.int32
    )
    for copy in near_copies:
        copy.wait()
    source = partner_base
    source_step = partner_step
    other_degree = inner_degree
    lane_msg = lax.broadcasted_iota(jnp.int32, (slots, MSG), 1)
    at_rank = lane_msg == rank * NQ
    for index, offset in enumerate(OFFSETS):
        from_here = peer_col == lax.rem(me + offset + parts, parts)
        far_degree = near[index, 2 * rows : 2 * rows + 16, :].astype(F32)[0:1, :]
        source = jnp.where(from_here, columns + index * MSG + rank * NQ, source)
        source_step = jnp.where(from_here, 1, source_step)
        other_degree = jnp.where(
            from_here, across(jnp.where(at_rank, far_degree, 0.0)), other_degree
        )
    live = peer_col >= 0
    turned = flag_col == 1
    source = jnp.where(turned, source + 7 * source_step, source)
    source_step = jnp.where(turned, -source_step, source_step)
    source = jnp.where(live, source, -1)
    source_step = jnp.where(live, source_step, 0)
    joint = jnp.maximum(degree_col, other_degree) + 1.0
    strength = jnp.where(live, PENALTY * joint * joint, 0.0)

    lane = lax.broadcasted_iota(jnp.int32, (slots, nodes), 1)
    owner = lax.shift_right_logical(lane, 3) == lax.broadcasted_iota(jnp.int32, (slots, nodes), 0)
    node = jnp.bitwise_and(lane, 7)
    own_line = down(jnp.where(owner, base_col + step_col * node, 0)).astype(jnp.int32)
    far_line = down(jnp.where(owner, source + source_step * node, 0)).astype(jnp.int32)
    factor = down(jnp.where(owner, strength, 0.0)) * weight_ref[...]
    factor_high = factor.astype(BF16).astype(F32)
    factor_low = factor - factor_high

    chunk = min(512, columns)
    for copy in copies:
        copy.wait()
    total_u = jnp.zeros((rows, nodes), F32)
    total_d = jnp.zeros((rows, nodes), F32)
    for start in range(0, columns, chunk):
        here = lax.broadcasted_iota(jnp.int32, (chunk, nodes), 0) + start
        pick = jnp.where(here == far_line, 1.0, 0.0).astype(BF16)
        total_u += dot(u_ref[:, start : start + chunk], pick)
        total_d += dot(d_ref[:, start : start + chunk], pick)
    for index in range(len(OFFSETS)):
        here = lax.broadcasted_iota(jnp.int32, (MSG, nodes), 0) + (columns + index * MSG)
        pick = jnp.where(here == far_line, 1.0, 0.0).astype(BF16)
        total_u += dot(near[index, 0:rows, :], pick)
        total_d += dot(near[index, rows : 2 * rows, :], pick)
    others[0:rows, :] = total_u.astype(BF16)
    others[rows : 2 * rows, :] = total_d.astype(BF16)
    others[2 * rows :, :] = jnp.ones((16, nodes), BF16)

    for start in range(0, columns, chunk):
        here = lax.broadcasted_iota(jnp.int32, (chunk, nodes), 0) + start
        match = here == own_line
        spread_high = jnp.where(match, factor_high, 0.0).astype(BF16)
        spread_low = jnp.where(match, factor_low, 0.0).astype(BF16)
        pulled = lax.dot_general(
            others[...], spread_high, NT, preferred_element_type=F32
        ) + lax.dot_general(others[...], spread_low, NT, preferred_element_type=F32)
        at = slice(start, start + chunk)
        scale = HELM_LAMBDA * mass_ref[:, at] + pulled[2 * rows : 2 * rows + 1, :]
        out_u[:, at] = scale * u_ref[:, at].astype(F32) - pulled[0:rows, :]
        out_d[:, at] = scale * d_ref[:, at].astype(F32) - pulled[rows : 2 * rows, :]


def finish_kernel(modes, rows, width, with_local, me_ref, *refs):
    fields = len(with_local)
    pieces = refs[:modes]
    refs = refs[modes:]
    count = sum(with_local)
    locals_in = refs[:count]
    outs = refs[count : count + fields]
    held, result, in_sem, out_sem = refs[count + fields :]
    me = me_ref[0]

    def at(d):
        return pl.ds(pl.multiple_of(jnp.bitwise_xor(me, d) * width, width), width)

    def load(i, d):
        return pltpu.make_async_copy(locals_in[i].at[:, at(d)], held.at[i, d], in_sem.at[i, d])

    def store(f, d):
        return pltpu.make_async_copy(result.at[f, d], outs[f].at[:, at(d)], out_sem.at[f, d])

    for d in range(modes):
        for i in range(count):
            load(i, d).start()
    for d in range(modes):
        seen = 0
        for f in range(fields):
            value = pieces[d][f].astype(F32)
            if with_local[f]:
                load(seen, d).wait()
                value = value + held[seen, d]
                seen += 1
            result[f, d] = value
            store(f, d).start()
    for d in range(modes):
        for f in range(fields):
            store(f, d).wait()


def finish(pieces, local, me):
    modes = len(pieces)
    fields, rows, width = pieces[0].shape
    with_local = tuple(part is not None for part in local)
    present = [part for part in local if part is not None]
    anywhere = pl.BlockSpec(memory_space=pl.ANY)
    return pl.pallas_call(
        functools.partial(finish_kernel, modes, rows, width, with_local),
        out_shape=[jax.ShapeDtypeStruct((rows, modes * width), F32)] * fields,
        in_specs=[SMEM] + [VMEM] * modes + [anywhere] * len(present),
        out_specs=[anywhere] * fields,
        scratch_shapes=[
            pltpu.VMEM((len(present), modes, rows, width), F32),
            pltpu.VMEM((fields, modes, rows, width), F32),
            pltpu.SemaphoreType.DMA((len(present), modes)),
            pltpu.SemaphoreType.DMA((fields, modes)),
        ],
        compiler_params=pltpu.CompilerParams(vmem_limit_bytes=16 * MIB),
        name="finish",
    )(me, *pieces, *present)


def swap_with(block, axis, distance):
    count = lax.axis_size(axis)
    return lax.ppermute(block, axis, [(i, i ^ distance) for i in range(count)])


def on_device(u_spec, dir_spec, advecting, viscosity, degrees, edge_side, edge_link):
    modes = lax.axis_size("mode")
    parts = lax.axis_size("elem")
    total, width = viscosity.shape
    rows, columns = u_spec.shape
    block_elements = degrees.shape[1] // modes
    slots = edge_side.shape[0]
    my_mode = lax.axis_index("mode")
    mode_id = my_mode.astype(jnp.int32).reshape(1)
    part_id = lax.axis_index("elem").astype(jnp.int32).reshape(1)

    derivative, weights = cheb_tables()
    identity = np.eye(block_elements)
    kron_x = np.kron(METRIC * derivative, np.eye(NQ * block_elements))
    group = width
    if width % 256 == 0 and 256 % (NQ * block_elements) == 0:
        group = 256
    kron_y = np.kron(np.eye(group // (NQ * block_elements)), np.kron(METRIC * derivative, identity))
    mass = np.repeat(AREA_SCALE * np.outer(weights, weights).reshape(-1), block_elements)
    synthesis, sloped = synthesis_tables(total)
    tables = [
        jnp.asarray(t)
        for t in (
            synthesis,
            sloped,
            np.ascontiguousarray(synthesis.T),
            np.ascontiguousarray(sloped.T),
            split_pair(kron_x.T),
            split_pair(kron_y.T),
            split_pair(kron_x),
            split_pair(kron_y),
        )
    ]
    mass_row = jnp.asarray(mass.astype(np.float32)[None, :])

    def cut(field):
        return [
            lax.dynamic_slice_in_dim(
                field, jnp.bitwise_xor(my_mode, d) * width, width, axis=1
            )
            for d in range(1, modes)
        ]

    order = [*range(2, modes), 1]
    u_cut = cut(u_spec)
    far = pl.BlockSpec(memory_space=pltpu.HBM)
    fields_held = [pltpu.VMEM((rows, columns), BF16)] * 2 + [pltpu.SemaphoreType.DMA((2,))]
    table_row = jnp.concatenate([edge_side[None, :], edge_link], axis=0)
    table_col = table_row.T
    table_row, table_col, u_cut = lax.optimization_barrier((table_row, table_col, u_cut))
    messages = pl.pallas_call(
        functools.partial(traces_kernel, parts, block_elements),
        out_shape=jax.ShapeDtypeStruct((parts, 2 * rows + 16, MSG), BF16),
        in_specs=[SMEM, far, far] + [VMEM] * 3,
        out_specs=VMEM,
        scratch_shapes=fields_held,
        compiler_params=pltpu.CompilerParams(vmem_limit_bytes=20 * MIB),
        name="traces",
    )(part_id, u_spec, dir_spec, table_row, table_col, degrees)

    u_pieces = [u_spec] + [None] * (modes - 1)
    for d in order:
        u_pieces[d] = swap_with(u_cut[d - 1], "mode", d)
    d_cut, u_pieces[1] = lax.optimization_barrier((cut(dir_spec), u_pieces[1]))
    d_pieces = [dir_spec] + [None] * (modes - 1)
    for d in order:
        d_pieces[d] = swap_with(d_cut[d - 1], "mode", d)

    u_pieces[1], messages = lax.optimization_barrier((u_pieces[1], messages))
    near = lax.all_to_all(messages, "elem", split_axis=0, concat_axis=0, tiled=True)
    u_back = planes(u_pieces, tables, viscosity, mass_row, advecting, mode_id)
    d_pieces[1], u_back = lax.optimization_barrier((d_pieces[1], list(u_back)))
    u_returned = [u_back[0]] + [None] * (modes - 1)
    for d in order:
        u_returned[d] = swap_with(u_back[d], "mode", d)
    d_back = planes(d_pieces, tables, viscosity, mass_row, None, mode_id)

    edge_weight = np.tile(LENGTH * weights, slots).astype(np.float32)[None, :]
    mass_local = np.tile(mass, modes).astype(np.float32)[None, :]
    local_u, local_d = pl.pallas_call(
        functools.partial(penalty_kernel, parts, block_elements),
        out_shape=[jax.ShapeDtypeStruct((rows, columns), F32)] * 2,
        in_specs=[SMEM, far, far] + [VMEM] * 6 + [far],
        out_specs=[VMEM] * 2,
        scratch_shapes=[pltpu.VMEM((2 * rows + 16, slots * NQ), BF16)]
        + fields_held
        + [
            pltpu.VMEM((len(OFFSETS), 2 * rows + 16, MSG), BF16),
            pltpu.SemaphoreType.DMA((len(OFFSETS),)),
        ],
        compiler_params=pltpu.CompilerParams(vmem_limit_bytes=32 * MIB),
        cost_estimate=pl.CostEstimate(
            flops=2 * 2 * rows * slots * NQ * 3 * columns,
            bytes_accessed=20 * rows * columns,
            transcendentals=0,
        ),
        name="penalty",
    )(
        part_id,
        u_spec,
        dir_spec,
        table_row,
        table_col,
        degrees,
        degrees.T,
        jnp.asarray(edge_weight),
        jnp.asarray(mass_local),
        near,
    )

    d_back, u_returned[1], local_d = lax.optimization_barrier((d_back, u_returned[1], local_d))
    d_returned = [d_back[0]] + [None] * (modes - 1)
    for d in order:
        d_returned[d] = swap_with(d_back[d], "mode", d)
    advect, helm_velocity = finish(u_returned, [None, local_u], mode_id)
    (helm_direction,) = finish(d_returned, [local_d], mode_id)
    return (advect, helm_velocity, helm_direction)


def solution(mesh):
    in_specs = (
        P("mode", "elem"),
        P("mode", "elem"),
        P(None, None, ("elem", "mode")),
        P(None, ("elem", "mode")),
        P(None, "elem"),
        P("elem"),
        P(None, "elem"),
    )
    out_specs = (P("mode", "elem"), P("mode", "elem"), P("mode", "elem"))
    return jax.shard_map(
        on_device, mesh=mesh, in_specs=in_specs, out_specs=out_specs, check_vma=False
    )
```

```python
import functools
import math

import jax
import jax.numpy as jnp
import ml_dtypes
import numpy as np
from jax import lax
from jax.experimental import pallas as pl
from jax.experimental.pallas import tpu as pltpu
from jax.sharding import PartitionSpec as P

NQ = 8
METRIC = 0.125
AREA_SCALE = 64.0
LENGTH = 8.0
HELM_LAMBDA = 4.0
PENALTY = 0.02
OFFSETS = (1, 2, -1, -2)
MSG = 256
MIB = 1024 * 1024
PLANES_LIMIT = 56

F32 = jnp.float32
BF16 = jnp.bfloat16
VMEM = pl.BlockSpec(memory_space=pltpu.VMEM)
SMEM = pl.BlockSpec(memory_space=pltpu.SMEM)
NT = (((1,), (1,)), ((), ()))


def cheb_tables():
    degree_top = 7
    angles = np.pi * np.arange(degree_top + 1) / degree_top
    cheb_points = np.cos(angles)
    signs_scale = np.ones(degree_top + 1)
    signs_scale[0] = 2.0
    signs_scale[degree_top] = 2.0
    signs_scale = signs_scale * (-1.0) ** np.arange(degree_top + 1)
    differences = cheb_points[:, None] - cheb_points[None, :]
    derivative = (
        signs_scale[:, None] / signs_scale[None, :] / (differences + np.eye(degree_top + 1))
    )
    derivative = derivative - np.eye(degree_top + 1) * derivative.sum(axis=1)[:, None]
    weights = np.zeros(degree_top + 1)
    interior = np.ones(degree_top - 1)
    for k in range(1, (degree_top - 1) // 2 + 1):
        interior = interior - 2.0 * np.cos(2 * k * angles[1:degree_top]) / (4 * k * k - 1)
    weights[0] = 1.0 / (degree_top * degree_top)
    weights[degree_top] = weights[0]
    weights[1:degree_top] = 2.0 * interior / degree_top
    return (derivative, weights)


def split_pair(matrix):
    matrix = matrix.astype(np.float32)
    high = matrix.astype(ml_dtypes.bfloat16)
    low = (matrix - high.astype(np.float32)).astype(ml_dtypes.bfloat16)
    return np.concatenate([high, high, low], axis=0)


def synthesis_tables(total):
    planes = np.arange(total)
    turn = (planes[:, None] * (planes // 2)[None, :]) % total
    angles = np.float32(2.0 * math.pi / total) * turn.astype(np.float32)
    angles = angles.astype(np.float64)
    table = np.where(planes[None, :] % 2 == 0, np.cos(angles), np.sin(angles))
    table = table * math.sqrt(2.0 / total)
    table[:, 0] = 1.0 / math.sqrt(total)
    table[:, 1] = (1 - 2 * (planes % 2)) / math.sqrt(total)
    rounded = table.astype(np.float32).astype(ml_dtypes.bfloat16)
    exact = rounded.astype(np.float64)
    rate = 4.0 / total * (planes[::2] // 2)
    sloped = np.zeros_like(exact)
    sloped[:, 1::2] = exact[:, 0::2] * rate[None, :]
    sloped[:, 0::2] = -exact[:, 1::2] * rate[None, :]
    return rounded, sloped.astype(np.float32).astype(ml_dtypes.bfloat16)


def shift_of(number):
    assert number & (number - 1) == 0
    return number.bit_length() - 1


def dot(a, b):
    return jnp.dot(a, b, preferred_element_type=F32)


def dot_split(value, table):
    high = value.astype(BF16)
    low = (value - high.astype(F32)).astype(BF16)
    return dot(jnp.concatenate([high, low, high], axis=1), table)


def planes_kernel(modes, chunk, advected, me_ref, *refs):
    own_ref, pieces = refs[0], refs[1:modes]
    s_in, sz_in, t_in, tz_in, *node_in = refs[modes : modes + 8]
    visc_in, mass_ref = refs[modes + 8 : modes + 10]
    refs = refs[modes + 10 :]
    if advected:
        adv_in, refs = refs[0], refs[1:]
    outs = refs[:modes]
    spec, flat, flux, s_ref, sz_ref, t_ref, tz_ref, visc_ref = refs[modes : modes + 8]
    rx_ref, ry_ref, kx_ref, ky_ref = node_refs = refs[modes + 8 : modes + 12]
    held, step_sem, node_sem, own_sem, back_sem, out_sem = refs[modes + 12 : modes + 18]
    if advected:
        moved, adv_ref = refs[modes + 18 :]
    me = me_ref[0]
    rows = own_ref.shape[0]
    total, width = visc_ref.shape
    group = ry_ref.shape[1]
    steps = total // chunk

    own_copy = pltpu.make_async_copy(
        own_ref.at[:, pl.ds(pl.multiple_of(me * width, width), width)],
        spec.at[pl.ds(pl.multiple_of(me * rows, rows), rows), :],
        own_sem,
    )
    node_copies = [
        pltpu.make_async_copy(source, target, node_sem.at[i])
        for i, (source, target) in enumerate(zip(node_in, node_refs))
    ]
    back_copies = [
        pltpu.make_async_copy(t_in, t_ref, back_sem.at[0]),
        pltpu.make_async_copy(tz_in, tz_ref, back_sem.at[1]),
    ]

    def plane_copies(step):
        at = pl.ds(pl.multiple_of(step * chunk, chunk), chunk)
        pairs = [(s_in, s_ref), (sz_in, sz_ref), (visc_in, visc_ref)]
        copies = [
            pltpu.make_async_copy(source.at[at, :], target.at[at, :], step_sem.at[step, i])
            for i, (source, target) in enumerate(pairs)
        ]
        if advected:
            copies.append(
                pltpu.make_async_copy(
                    adv_in.at[:, at, :], adv_ref.at[:, at, :], step_sem.at[step, 3]
                )
            )
        return copies

    own_copy.start()
    first = plane_copies(0)
    for copy in first[:2] + node_copies[:2] + first[2:] + node_copies[2:]:
        copy.start()
    for step in range(1, steps):
        for copy in plane_copies(step):
            copy.start()
    for copy in back_copies:
        copy.start()
    for d in range(1, modes):
        at = pl.ds(pl.multiple_of(jnp.bitwise_xor(me, d) * rows, rows), rows)
        spec[at, :] = pieces[d - 1][...]
    own_copy.wait()

    def grouped(value, ref):
        parts = [
            dot_split(value[:, g : g + group], ref[...]) for g in range(0, width, group)
        ]
        return parts[0] if len(parts) == 1 else jnp.concatenate(parts, axis=1)

    def forward(step, carry):
        at = pl.ds(pl.multiple_of(step * chunk, chunk), chunk)
        copies = plane_copies(step)
        for copy in copies[:2]:
            copy.wait()
        coeffs = spec[...]
        plain = dot(s_ref[at, :], coeffs)
        along = dot(sz_ref[at, :], coeffs)

        @pl.when(step == 0)
        def _():
            for copy in node_copies:
                copy.wait()

        for copy in copies[2:]:
            copy.wait()
        grad_x = dot_split(plain, rx_ref[...])
        grad_y = grouped(plain, ry_ref)
        weighted = mass_ref[...] * visc_ref[at, :].astype(F32)
        if advected:
            moved[at, :] = (
                adv_ref[0, at, :].astype(F32) * grad_x
                + adv_ref[1, at, :].astype(F32) * grad_y
                + adv_ref[2, at, :].astype(F32) * along
            ).astype(BF16)
        flux[at, :] = (weighted * along).astype(BF16)
        flat_sum = dot_split(weighted * grad_x, kx_ref[...]) + grouped(weighted * grad_y, ky_ref)
        flat[at, :] = flat_sum.astype(BF16)
        return carry

    lax.fori_loop(0, steps, forward, 0)

    for copy in back_copies:
        copy.wait()
    stores = [pltpu.make_async_copy(held.at[d], outs[d], out_sem.at[d]) for d in range(modes)]
    for d in [*range(1, modes), 0]:
        at = pl.ds(pl.multiple_of(jnp.bitwise_xor(me, d) * rows, rows), rows)
        volume = dot(t_ref[at, :], flat[...]) + dot(tz_ref[at, :], flux[...])
        if advected:
            held[d, 0] = dot(t_ref[at, :], moved[...]).astype(BF16)
            held[d, 1] = volume.astype(BF16)
        else:
            held[d, 0] = volume.astype(BF16)
        stores[d].start()
    for store in stores:
        store.wait()


def planes(pieces, tables, visc, mass, adv, me):
    modes = len(pieces)
    rows = pieces[0].shape[0]
    total, width = visc.shape
    group = tables[5].shape[1]
    chunk = min(256, total)
    advected = adv is not None
    fields = 2 if advected else 1
    operands = [me, *pieces, *tables, visc, mass] + ([adv] if advected else [])
    flops = 2 * total * total * width * (2 + 2 + (1 if advected else 0))
    flops += 2 * total * width * width * 9
    far = pl.BlockSpec(memory_space=pltpu.HBM)
    plane = pltpu.VMEM((total, width), BF16)
    square = pltpu.VMEM((total, total), BF16)
    node_x = pltpu.VMEM((3 * width, width), BF16)
    node_y = pltpu.VMEM((3 * group, group), BF16)
    scratch = [plane] * 3 + [square] * 4 + [plane, node_x, node_y, node_x, node_y]
    scratch += [
        pltpu.VMEM((modes, fields, rows, width), BF16),
        pltpu.SemaphoreType.DMA((total // chunk, 4)),
        pltpu.SemaphoreType.DMA((4,)),
        pltpu.SemaphoreType.DMA,
        pltpu.SemaphoreType.DMA((2,)),
        pltpu.SemaphoreType.DMA((modes,)),
    ]
    if advected:
        scratch += [plane, pltpu.VMEM(adv.shape, BF16)]
    return pl.pallas_call(
        functools.partial(planes_kernel, modes, chunk, advected),
        out_shape=[jax.ShapeDtypeStruct((fields, rows, width), BF16)] * modes,
        in_specs=[SMEM, far]
        + [VMEM] * (modes - 1)
        + [far] * (len(tables) + 1)
        + [VMEM]
        + [far] * (1 if advected else 0),
        out_specs=[far] * modes,
        scratch_shapes=scratch,
        compiler_params=pltpu.CompilerParams(vmem_limit_bytes=PLANES_LIMIT * MIB),
        cost_estimate=pl.CostEstimate(
            flops=flops, bytes_accessed=12 * total * total, transcendentals=0
        ),
        name="planes_moved" if advected else "planes_plain",
    )(*operands)


def slot_line(side, block_elements):
    element = lax.shift_right_logical(side, 2)
    code = jnp.bitwise_and(side, 3)
    first = jnp.where(code == 0, 0, jnp.where(code == 1, 7, jnp.where(code == 2, 63, 56)))
    step = jnp.where(code == 0, 1, jnp.where(code == 1, 8, jnp.where(code == 2, -1, -8)))
    block = lax.shift_right_logical(element, shift_of(block_elements))
    inner = jnp.bitwise_and(element, block_elements - 1)
    base = block * (NQ * NQ * block_elements) + first * block_elements + inner
    return base, step * block_elements


def across(values):
    return jnp.sum(values.astype(F32), axis=1, keepdims=True)


def down(values):
    return jnp.sum(values.astype(F32), axis=0, keepdims=True)


def degree_column(side_col, degrees):
    slots = side_col.shape[0]
    elements = degrees.shape[1]
    lanes = lax.broadcasted_iota(jnp.int32, (slots, elements), 1)
    mine = lanes == lax.shift_right_logical(side_col, 2)
    along_x = jnp.bitwise_and(side_col, 1) == 0
    value = jnp.where(along_x, degrees[0:1, :], degrees[1:2, :])
    return across(jnp.where(mine, value, 0))


def fetch(source, target, sem):
    return pltpu.make_async_copy(source, target, sem)


def traces_kernel(parts, block_elements, me_ref, u_in, d_in, row_ref, col_ref, deg_ref, *refs):
    out, u_ref, d_ref, sem = refs
    copies = [fetch(u_in, u_ref, sem.at[0]), fetch(d_in, d_ref, sem.at[1])]
    for copy in copies:
        copy.start()
    me = me_ref[0]
    rows, columns = u_ref.shape
    side_col = col_ref[:, 0:1]
    peer_col = col_ref[:, 2:3]
    peer_row = row_ref[2:3, :]
    slots = side_col.shape[0]
    base, step = slot_line(side_col, block_elements)
    degree = degree_column(side_col, deg_ref[...])
    before = lax.broadcasted_iota(jnp.int32, (slots, slots), 1) < lax.broadcasted_iota(
        jnp.int32, (slots, slots), 0
    )
    lane = lax.broadcasted_iota(jnp.int32, (slots, MSG), 1)
    place = lax.shift_right_logical(lane, 3)
    line = base + step * jnp.bitwise_and(lane, 7) + 1
    chunk = min(512, columns)
    for copy in copies:
        copy.wait()
    for offset in OFFSETS:
        peer = lax.rem(me + offset + parts, parts)
        rank = across(jnp.where((peer_row == peer) & before, 1, 0)).astype(jnp.int32)
        chosen = (peer_col == peer) & (rank == place)
        target = down(jnp.where(chosen, line, 0)).astype(jnp.int32) - 1
        total_u = jnp.zeros((rows, MSG), F32)
        total_d = jnp.zeros((rows, MSG), F32)
        for start in range(0, columns, chunk):
            here = lax.broadcasted_iota(jnp.int32, (chunk, MSG), 0) + start
            pick = jnp.where(here == target, 1.0, 0.0).astype(BF16)
            total_u += dot(u_ref[:, start : start + chunk], pick)
            total_d += dot(d_ref[:, start : start + chunk], pick)
        out[peer, 0:rows, :] = total_u.astype(BF16)
        out[peer, rows : 2 * rows, :] = total_d.astype(BF16)
        degrees = down(jnp.where(chosen, degree, 0.0))
        out[peer, 2 * rows :, :] = jnp.broadcast_to(degrees, (16, MSG)).astype(BF16)


def penalty_kernel(
    parts,
    block_elements,
    me_ref,
    u_in,
    d_in,
    row_ref,
    col_ref,
    deg_ref,
    degt_ref,
    weight_ref,
    mass_ref,
    near_in,
    out_u,
    out_d,
    others,
    u_ref,
    d_ref,
    sem,
    near,
    near_sem,
):
    me = me_ref[0]
    near_copies = [
        fetch(near_in.at[lax.rem(me + offset + parts, parts)], near.at[i], near_sem.at[i])
        for i, offset in enumerate(OFFSETS)
    ]
    copies = [fetch(u_in, u_ref, sem.at[0]), fetch(d_in, d_ref, sem.at[1])]
    for copy in near_copies + copies:
        copy.start()
    rows, columns = u_ref.shape
    side_col, flag_col, peer_col, slot_col = (col_ref[:, i : i + 1] for i in range(4))
    side_row, peer_row, slot_row = row_ref[0:1, :], row_ref[2:3, :], row_ref[3:4, :]
    slots = side_col.shape[0]
    nodes = slots * NQ
    base_col, step_col = slot_line(side_col, block_elements)
    base_row, step_row = slot_line(side_row, block_elements)
    degree_col = degree_column(side_col, deg_ref[...])
    elements = degt_ref.shape[0]
    level = lax.broadcasted_iota(jnp.int32, (elements, slots), 0)
    mine = level == lax.shift_right_logical(side_row, 2)
    value = jnp.where(jnp.bitwise_and(side_row, 1) == 0, degt_ref[:, 0:1], degt_ref[:, 1:2])
    degree_row = down(jnp.where(mine, value, 0))

    lane_slot = lax.broadcasted_iota(jnp.int32, (slots, slots), 1)
    partner = lane_slot == slot_col
    partner_base = across(jnp.where(partner, base_row, 0)).astype(jnp.int32)
    partner_step = across(jnp.where(partner, step_row, 0)).astype(jnp.int32)
    inner_degree = across(jnp.where(partner, degree_row, 0.0))
    rank = across(jnp.where((peer_row == peer_col) & (slot_row < slot_col), 1, 0)).astype(
        jnp.int32
    )
    for copy in near_copies:
        copy.wait()
    source = partner_base
    source_step = partner_step
    other_degree = inner_degree
    lane_msg = lax.broadcasted_iota(jnp.int32, (slots, MSG), 1)
    at_rank = lane_msg == rank * NQ
    for index, offset in enumerate(OFFSETS):
        from_here = peer_col == lax.rem(me + offset + parts, parts)
        far_degree = near[index, 2 * rows : 2 * rows + 16, :].astype(F32)[0:1, :]
        source = jnp.where(from_here, columns + index * MSG + rank * NQ, source)
        source_step = jnp.where(from_here, 1, source_step)
        other_degree = jnp.where(
            from_here, across(jnp.where(at_rank, far_degree, 0.0)), other_degree
        )
    live = peer_col >= 0
    turned = flag_col == 1
    source = jnp.where(turned, source + 7 * source_step, source)
    source_step = jnp.where(turned, -source_step, source_step)
    source = jnp.where(live, source, -1)
    source_step = jnp.where(live, source_step, 0)
    joint = jnp.maximum(degree_col, other_degree) + 1.0
    strength = jnp.where(live, PENALTY * joint * joint, 0.0)

    lane = lax.broadcasted_iota(jnp.int32, (slots, nodes), 1)
    owner = lax.shift_right_logical(lane, 3) == lax.broadcasted_iota(jnp.int32, (slots, nodes), 0)
    node = jnp.bitwise_and(lane, 7)
    own_line = down(jnp.where(owner, base_col + step_col * node, 0)).astype(jnp.int32)
    far_line = down(jnp.where(owner, source + source_step * node, 0)).astype(jnp.int32)
    factor = down(jnp.where(owner, strength, 0.0)) * weight_ref[...]
    factor_high = factor.astype(BF16).astype(F32)
    factor_low = factor - factor_high

    chunk = min(512, columns)
    for copy in copies:
        copy.wait()
    total_u = jnp.zeros((rows, nodes), F32)
    total_d = jnp.zeros((rows, nodes), F32)
    for start in range(0, columns, chunk):
        here = lax.broadcasted_iota(jnp.int32, (chunk, nodes), 0) + start
        pick = jnp.where(here == far_line, 1.0, 0.0).astype(BF16)
        total_u += dot(u_ref[:, start : start + chunk], pick)
        total_d += dot(d_ref[:, start : start + chunk], pick)
    for index in range(len(OFFSETS)):
        here = lax.broadcasted_iota(jnp.int32, (MSG, nodes), 0) + (columns + index * MSG)
        pick = jnp.where(here == far_line, 1.0, 0.0).astype(BF16)
        total_u += dot(near[index, 0:rows, :], pick)
        total_d += dot(near[index, rows : 2 * rows, :], pick)
    others[0:rows, :] = total_u.astype(BF16)
    others[rows : 2 * rows, :] = total_d.astype(BF16)
    others[2 * rows :, :] = jnp.ones((16, nodes), BF16)

    for start in range(0, columns, chunk):
        here = lax.broadcasted_iota(jnp.int32, (chunk, nodes), 0) + start
        match = here == own_line
        spread_high = jnp.where(match, factor_high, 0.0).astype(BF16)
        spread_low = jnp.where(match, factor_low, 0.0).astype(BF16)
        pulled = lax.dot_general(
            others[...], spread_high, NT, preferred_element_type=F32
        ) + lax.dot_general(others[...], spread_low, NT, preferred_element_type=F32)
        at = slice(start, start + chunk)
        scale = HELM_LAMBDA * mass_ref[:, at] + pulled[2 * rows : 2 * rows + 1, :]
        out_u[:, at] = scale * u_ref[:, at].astype(F32) - pulled[0:rows, :]
        out_d[:, at] = scale * d_ref[:, at].astype(F32) - pulled[rows : 2 * rows, :]


def finish_kernel(modes, width, with_local, me_ref, *refs):
    fields = len(with_local)
    count = sum(with_local)
    pieces, refs = refs[:modes], refs[modes:]
    locals_in, outs = refs[:count], refs[count : count + fields]
    result, sem = refs[count + fields :]
    me = me_ref[0]

    def at(d):
        return pl.ds(pl.multiple_of(jnp.bitwise_xor(me, d) * width, width), width)

    stores = []
    for d in range(modes):
        seen = 0
        for f in range(fields):
            value = pieces[d][f].astype(F32)
            if with_local[f]:
                value = value + locals_in[seen][:, at(d)]
                seen += 1
            result[f, d] = value
            stores.append(pltpu.make_async_copy(result.at[f, d], outs[f].at[:, at(d)], sem.at[f, d]))
            stores[-1].start()
    for store in stores:
        store.wait()


def finish(pieces, local, me):
    modes = len(pieces)
    fields, rows, width = pieces[0].shape
    with_local = tuple(part is not None for part in local)
    present = [part for part in local if part is not None]
    return pl.pallas_call(
        functools.partial(finish_kernel, modes, width, with_local),
        out_shape=[jax.ShapeDtypeStruct((rows, modes * width), F32)] * fields,
        in_specs=[SMEM] + [VMEM] * (modes + len(present)),
        out_specs=[pl.BlockSpec(memory_space=pl.ANY)] * fields,
        scratch_shapes=[
            pltpu.VMEM((fields, modes, rows, width), F32),
            pltpu.SemaphoreType.DMA((fields, modes)),
        ],
        compiler_params=pltpu.CompilerParams(vmem_limit_bytes=16 * MIB),
        name="finish",
    )(me, *pieces, *present)


def swap_with(block, axis, distance):
    count = lax.axis_size(axis)
    return lax.ppermute(block, axis, [(i, i ^ distance) for i in range(count)])


def on_device(u_spec, dir_spec, advecting, viscosity, degrees, edge_side, edge_link):
    modes = lax.axis_size("mode")
    parts = lax.axis_size("elem")
    total, width = viscosity.shape
    rows, columns = u_spec.shape
    block_elements = degrees.shape[1] // modes
    slots = edge_side.shape[0]
    my_mode = lax.axis_index("mode")
    mode_id = my_mode.astype(jnp.int32).reshape(1)
    part_id = lax.axis_index("elem").astype(jnp.int32).reshape(1)

    derivative, weights = cheb_tables()
    identity = np.eye(block_elements)
    kron_x = np.kron(METRIC * derivative, np.eye(NQ * block_elements))
    group = width
    if width % 256 == 0 and 256 % (NQ * block_elements) == 0:
        group = 256
    kron_y = np.kron(np.eye(group // (NQ * block_elements)), np.kron(METRIC * derivative, identity))
    mass = np.repeat(AREA_SCALE * np.outer(weights, weights).reshape(-1), block_elements)
    synthesis, sloped = synthesis_tables(total)
    tables = [
        jnp.asarray(t)
        for t in (
            synthesis,
            sloped,
            np.ascontiguousarray(synthesis.T),
            np.ascontiguousarray(sloped.T),
            split_pair(kron_x.T),
            split_pair(kron_y.T),
            split_pair(kron_x),
            split_pair(kron_y),
        )
    ]
    mass_row = jnp.asarray(mass.astype(np.float32)[None, :])

    def cut(field):
        return [
            lax.dynamic_slice_in_dim(
                field, jnp.bitwise_xor(my_mode, d) * width, width, axis=1
            )
            for d in range(1, modes)
        ]

    order = [*range(2, modes), 1]
    u_cut = cut(u_spec)
    far = pl.BlockSpec(memory_space=pltpu.HBM)
    fields_held = [pltpu.VMEM((rows, columns), BF16)] * 2 + [pltpu.SemaphoreType.DMA((2,))]
    edge_side, edge_link, u_cut = lax.optimization_barrier((edge_side, edge_link, u_cut))
    table_row = jnp.concatenate([edge_side[None, :], edge_link], axis=0)
    table_col = table_row.T
    messages = pl.pallas_call(
        functools.partial(traces_kernel, parts, block_elements),
        out_shape=jax.ShapeDtypeStruct((parts, 2 * rows + 16, MSG), BF16),
        in_specs=[SMEM, far, far] + [VMEM] * 3,
        out_specs=VMEM,
        scratch_shapes=fields_held,
        compiler_params=pltpu.CompilerParams(vmem_limit_bytes=20 * MIB),
        name="traces",
    )(part_id, u_spec, dir_spec, table_row, table_col, degrees)

    u_pieces = [u_spec] + [None] * (modes - 1)
    for d in order:
        u_pieces[d] = swap_with(u_cut[d - 1], "mode", d)
    d_cut, u_pieces[1] = lax.optimization_barrier((cut(dir_spec), u_pieces[1]))
    d_pieces = [dir_spec] + [None] * (modes - 1)
    for d in order:
        d_pieces[d] = swap_with(d_cut[d - 1], "mode", d)

    u_pieces[1], messages = lax.optimization_barrier((u_pieces[1], messages))
    near = lax.all_to_all(messages, "elem", split_axis=0, concat_axis=0, tiled=True)
    u_back = planes(u_pieces, tables, viscosity, mass_row, advecting, mode_id)
    d_pieces[1], u_back = lax.optimization_barrier((d_pieces[1], list(u_back)))
    u_returned = [u_back[0]] + [None] * (modes - 1)
    for d in order:
        u_returned[d] = swap_with(u_back[d], "mode", d)
    d_back = planes(d_pieces, tables, viscosity, mass_row, None, mode_id)

    edge_weight = np.tile(LENGTH * weights, slots).astype(np.float32)[None, :]
    mass_local = np.tile(mass, modes).astype(np.float32)[None, :]
    local_u, local_d = pl.pallas_call(
        functools.partial(penalty_kernel, parts, block_elements),
        out_shape=[jax.ShapeDtypeStruct((rows, columns), F32)] * 2,
        in_specs=[SMEM, far, far] + [VMEM] * 6 + [far],
        out_specs=[VMEM] * 2,
        scratch_shapes=[pltpu.VMEM((2 * rows + 16, slots * NQ), BF16)]
        + fields_held
        + [
            pltpu.VMEM((len(OFFSETS), 2 * rows + 16, MSG), BF16),
            pltpu.SemaphoreType.DMA((len(OFFSETS),)),
        ],
        compiler_params=pltpu.CompilerParams(vmem_limit_bytes=32 * MIB),
        cost_estimate=pl.CostEstimate(
            flops=2 * 2 * rows * slots * NQ * 3 * columns,
            bytes_accessed=20 * rows * columns,
            transcendentals=0,
        ),
        name="penalty",
    )(
        part_id,
        u_spec,
        dir_spec,
        table_row,
        table_col,
        degrees,
        degrees.T,
        jnp.asarray(edge_weight),
        jnp.asarray(mass_local),
        near,
    )

    d_back, u_returned[1], local_d = lax.optimization_barrier((d_back, u_returned[1], local_d))
    d_returned = [d_back[0]] + [None] * (modes - 1)
    for d in order:
        d_returned[d] = swap_with(d_back[d], "mode", d)
    advect, helm_velocity = finish(u_returned, [None, local_u], mode_id)
    (helm_direction,) = finish(d_returned, [local_d], mode_id)
    return (advect, helm_velocity, helm_direction)


def solution(mesh):
    in_specs = (
        P("mode", "elem"),
        P("mode", "elem"),
        P(None, None, ("elem", "mode")),
        P(None, ("elem", "mode")),
        P(None, "elem"),
        P("elem"),
        P(None, "elem"),
    )
    out_specs = (P("mode", "elem"), P("mode", "elem"), P("mode", "elem"))
    return jax.shard_map(
        on_device, mesh=mesh, in_specs=in_specs, out_specs=out_specs, check_vma=False
    )
```

```python
import functools
import math

import jax
import jax.numpy as jnp
import ml_dtypes
import numpy as np
from jax import lax
from jax.experimental import pallas as pl
from jax.experimental.pallas import tpu as pltpu
from jax.sharding import PartitionSpec as P

NQ = 8
METRIC = 0.125
AREA_SCALE = 64.0
LENGTH = 8.0
HELM_LAMBDA = 4.0
PENALTY = 0.02
OFFSETS = (1, 2, -1, -2)
MSG = 256
MIB = 1024 * 1024
PLANES_LIMIT = 56

F32 = jnp.float32
BF16 = jnp.bfloat16
VMEM = pl.BlockSpec(memory_space=pltpu.VMEM)
SMEM = pl.BlockSpec(memory_space=pltpu.SMEM)
NT = (((1,), (1,)), ((), ()))


def cheb_tables():
    degree_top = 7
    angles = np.pi * np.arange(degree_top + 1) / degree_top
    cheb_points = np.cos(angles)
    signs_scale = np.ones(degree_top + 1)
    signs_scale[0] = 2.0
    signs_scale[degree_top] = 2.0
    signs_scale = signs_scale * (-1.0) ** np.arange(degree_top + 1)
    differences = cheb_points[:, None] - cheb_points[None, :]
    derivative = (
        signs_scale[:, None] / signs_scale[None, :] / (differences + np.eye(degree_top + 1))
    )
    derivative = derivative - np.eye(degree_top + 1) * derivative.sum(axis=1)[:, None]
    weights = np.zeros(degree_top + 1)
    interior = np.ones(degree_top - 1)
    for k in range(1, (degree_top - 1) // 2 + 1):
        interior = interior - 2.0 * np.cos(2 * k * angles[1:degree_top]) / (4 * k * k - 1)
    weights[0] = 1.0 / (degree_top * degree_top)
    weights[degree_top] = weights[0]
    weights[1:degree_top] = 2.0 * interior / degree_top
    return (derivative, weights)


def split_pair(matrix):
    matrix = matrix.astype(np.float32)
    high = matrix.astype(ml_dtypes.bfloat16)
    low = (matrix - high.astype(np.float32)).astype(ml_dtypes.bfloat16)
    return np.concatenate([high, high, low], axis=0)


def synthesis_tables(total):
    planes = np.arange(total)
    turn = (planes[:, None] * (planes // 2)[None, :]) % total
    angles = np.float32(2.0 * math.pi / total) * turn.astype(np.float32)
    angles = angles.astype(np.float64)
    table = np.where(planes[None, :] % 2 == 0, np.cos(angles), np.sin(angles))
    table = table * math.sqrt(2.0 / total)
    table[:, 0] = 1.0 / math.sqrt(total)
    table[:, 1] = (1 - 2 * (planes % 2)) / math.sqrt(total)
    rounded = table.astype(np.float32).astype(ml_dtypes.bfloat16)
    exact = rounded.astype(np.float64)
    rate = 4.0 / total * (planes[::2] // 2)
    sloped = np.zeros_like(exact)
    sloped[:, 1::2] = exact[:, 0::2] * rate[None, :]
    sloped[:, 0::2] = -exact[:, 1::2] * rate[None, :]
    return rounded, sloped.astype(np.float32).astype(ml_dtypes.bfloat16)


def shift_of(number):
    assert number & (number - 1) == 0
    return number.bit_length() - 1


def dot(a, b):
    return jnp.dot(a, b, preferred_element_type=F32)


def dot_split(value, table):
    high = value.astype(BF16)
    low = (value - high.astype(F32)).astype(BF16)
    return dot(jnp.concatenate([high, low, high], axis=1), table)


def cut_kernel(modes, me_ref, field, *refs):
    pieces, sem = refs[:-1], refs[-1]
    me = me_ref[0]
    width = pieces[0].shape[1]
    copies = []
    for d in range(1, modes):
        at = pl.ds(pl.multiple_of(jnp.bitwise_xor(me, d) * width, width), width)
        copies.append(pltpu.make_async_copy(field.at[:, at], pieces[d - 1], sem.at[d - 1]))
        copies[-1].start()
    for copy in copies:
        copy.wait()


def planes_kernel(modes, chunk, advected, me_ref, *refs):
    own_ref, pieces = refs[0], refs[1:modes]
    s_in, sz_in, t_in, tz_in, *node_in = refs[modes : modes + 8]
    visc_in, mass_ref = refs[modes + 8 : modes + 10]
    refs = refs[modes + 10 :]
    if advected:
        adv_in, refs = refs[0], refs[1:]
    outs = refs[:modes]
    spec, flat, flux, s_ref, sz_ref, t_ref, tz_ref, visc_ref = refs[modes : modes + 8]
    rx_ref, ry_ref, kx_ref, ky_ref = node_refs = refs[modes + 8 : modes + 12]
    held, step_sem, node_sem, own_sem, back_sem, out_sem = refs[modes + 12 : modes + 18]
    if advected:
        moved, adv_ref = refs[modes + 18 :]
    me = me_ref[0]
    rows = own_ref.shape[0]
    total, width = visc_ref.shape
    group = ry_ref.shape[1]
    steps = total // chunk

    own_copy = pltpu.make_async_copy(
        own_ref.at[:, pl.ds(pl.multiple_of(me * width, width), width)],
        spec.at[pl.ds(pl.multiple_of(me * rows, rows), rows), :],
        own_sem,
    )
    node_copies = [
        pltpu.make_async_copy(source, target, node_sem.at[i])
        for i, (source, target) in enumerate(zip(node_in, node_refs))
    ]
    back_copies = [
        pltpu.make_async_copy(t_in, t_ref, back_sem.at[0]),
        pltpu.make_async_copy(tz_in, tz_ref, back_sem.at[1]),
    ]

    def plane_copies(step):
        at = pl.ds(pl.multiple_of(step * chunk, chunk), chunk)
        pairs = [(s_in, s_ref), (sz_in, sz_ref), (visc_in, visc_ref)]
        copies = [
            pltpu.make_async_copy(source.at[at, :], target.at[at, :], step_sem.at[step, i])
            for i, (source, target) in enumerate(pairs)
        ]
        if advected:
            copies.append(
                pltpu.make_async_copy(
                    adv_in.at[:, at, :], adv_ref.at[:, at, :], step_sem.at[step, 3]
                )
            )
        return copies

    own_copy.start()
    first = plane_copies(0)
    for copy in first[:2] + node_copies[:2] + first[2:] + node_copies[2:]:
        copy.start()
    for step in range(1, steps):
        for copy in plane_copies(step):
            copy.start()
    for copy in back_copies:
        copy.start()
    for d in range(1, modes):
        at = pl.ds(pl.multiple_of(jnp.bitwise_xor(me, d) * rows, rows), rows)
        spec[at, :] = pieces[d - 1][...]
    own_copy.wait()

    def grouped(value, ref):
        parts = [
            dot_split(value[:, g : g + group], ref[...]) for g in range(0, width, group)
        ]
        return parts[0] if len(parts) == 1 else jnp.concatenate(parts, axis=1)

    def forward(step, carry):
        at = pl.ds(pl.multiple_of(step * chunk, chunk), chunk)
        copies = plane_copies(step)
        for copy in copies[:2]:
            copy.wait()
        coeffs = spec[...]
        plain = dot(s_ref[at, :], coeffs)
        along = dot(sz_ref[at, :], coeffs)

        @pl.when(step == 0)
        def _():
            for copy in node_copies:
                copy.wait()

        for copy in copies[2:]:
            copy.wait()
        grad_x = dot_split(plain, rx_ref[...])
        grad_y = grouped(plain, ry_ref)
        weighted = mass_ref[...] * visc_ref[at, :].astype(F32)
        if advected:
            moved[at, :] = (
                adv_ref[0, at, :].astype(F32) * grad_x
                + adv_ref[1, at, :].astype(F32) * grad_y
                + adv_ref[2, at, :].astype(F32) * along
            ).astype(BF16)
        flux[at, :] = (weighted * along).astype(BF16)
        flat_sum = dot_split(weighted * grad_x, kx_ref[...]) + grouped(weighted * grad_y, ky_ref)
        flat[at, :] = flat_sum.astype(BF16)
        return carry

    lax.fori_loop(0, steps, forward, 0)

    for copy in back_copies:
        copy.wait()
    stores = [pltpu.make_async_copy(held.at[d], outs[d], out_sem.at[d]) for d in range(modes)]
    for d in [*range(1, modes), 0]:
        at = pl.ds(pl.multiple_of(jnp.bitwise_xor(me, d) * rows, rows), rows)
        volume = dot(t_ref[at, :], flat[...]) + dot(tz_ref[at, :], flux[...])
        if advected:
            held[d, 0] = dot(t_ref[at, :], moved[...]).astype(BF16)
            held[d, 1] = volume.astype(BF16)
        else:
            held[d, 0] = volume.astype(BF16)
        stores[d].start()
    for store in stores:
        store.wait()


def planes(pieces, tables, visc, mass, adv, me):
    modes = len(pieces)
    rows = pieces[0].shape[0]
    total, width = visc.shape
    group = tables[5].shape[1]
    chunk = min(256, total)
    advected = adv is not None
    fields = 2 if advected else 1
    operands = [me, *pieces, *tables, visc, mass] + ([adv] if advected else [])
    flops = 2 * total * total * width * (2 + 2 + (1 if advected else 0))
    flops += 2 * total * width * width * 9
    far = pl.BlockSpec(memory_space=pltpu.HBM)
    plane = pltpu.VMEM((total, width), BF16)
    square = pltpu.VMEM((total, total), BF16)
    node_x = pltpu.VMEM((3 * width, width), BF16)
    node_y = pltpu.VMEM((3 * group, group), BF16)
    scratch = [plane] * 3 + [square] * 4 + [plane, node_x, node_y, node_x, node_y]
    scratch += [
        pltpu.VMEM((modes, fields, rows, width), BF16),
        pltpu.SemaphoreType.DMA((total // chunk, 4)),
        pltpu.SemaphoreType.DMA((4,)),
        pltpu.SemaphoreType.DMA,
        pltpu.SemaphoreType.DMA((2,)),
        pltpu.SemaphoreType.DMA((modes,)),
    ]
    if advected:
        scratch += [plane, pltpu.VMEM(adv.shape, BF16)]
    return pl.pallas_call(
        functools.partial(planes_kernel, modes, chunk, advected),
        out_shape=[jax.ShapeDtypeStruct((fields, rows, width), BF16)] * modes,
        in_specs=[SMEM, far]
        + [VMEM] * (modes - 1)
        + [far] * (len(tables) + 1)
        + [VMEM]
        + [far] * (1 if advected else 0),
        out_specs=[far] * modes,
        scratch_shapes=scratch,
        compiler_params=pltpu.CompilerParams(vmem_limit_bytes=PLANES_LIMIT * MIB),
        cost_estimate=pl.CostEstimate(
            flops=flops, bytes_accessed=12 * total * total, transcendentals=0
        ),
        name="planes_moved" if advected else "planes_plain",
    )(*operands)


def slot_line(side, block_elements):
    element = lax.shift_right_logical(side, 2)
    code = jnp.bitwise_and(side, 3)
    first = jnp.where(code == 0, 0, jnp.where(code == 1, 7, jnp.where(code == 2, 63, 56)))
    step = jnp.where(code == 0, 1, jnp.where(code == 1, 8, jnp.where(code == 2, -1, -8)))
    block = lax.shift_right_logical(element, shift_of(block_elements))
    inner = jnp.bitwise_and(element, block_elements - 1)
    base = block * (NQ * NQ * block_elements) + first * block_elements + inner
    return base, step * block_elements


def across(values):
    return jnp.sum(values.astype(F32), axis=1, keepdims=True)


def down(values):
    return jnp.sum(values.astype(F32), axis=0, keepdims=True)


def degree_column(side_col, degrees):
    slots = side_col.shape[0]
    elements = degrees.shape[1]
    lanes = lax.broadcasted_iota(jnp.int32, (slots, elements), 1)
    mine = lanes == lax.shift_right_logical(side_col, 2)
    along_x = jnp.bitwise_and(side_col, 1) == 0
    value = jnp.where(along_x, degrees[0:1, :], degrees[1:2, :])
    return across(jnp.where(mine, value, 0))


def fetch(source, target, sem):
    return pltpu.make_async_copy(source, target, sem)


def traces_kernel(parts, block_elements, me_ref, u_in, d_in, row_ref, col_ref, deg_ref, *refs):
    out, u_ref, d_ref, sem = refs
    copies = [fetch(u_in, u_ref, sem.at[0]), fetch(d_in, d_ref, sem.at[1])]
    for copy in copies:
        copy.start()
    me = me_ref[0]
    rows, columns = u_ref.shape
    side_col = col_ref[:, 0:1]
    peer_col = col_ref[:, 2:3]
    peer_row = row_ref[2:3, :]
    slots = side_col.shape[0]
    base, step = slot_line(side_col, block_elements)
    degree = degree_column(side_col, deg_ref[...])
    before = lax.broadcasted_iota(jnp.int32, (slots, slots), 1) < lax.broadcasted_iota(
        jnp.int32, (slots, slots), 0
    )
    lane = lax.broadcasted_iota(jnp.int32, (slots, MSG), 1)
    place = lax.shift_right_logical(lane, 3)
    line = base + step * jnp.bitwise_and(lane, 7) + 1
    chunk = min(512, columns)
    for copy in copies:
        copy.wait()
    for offset in OFFSETS:
        peer = lax.rem(me + offset + parts, parts)
        rank = across(jnp.where((peer_row == peer) & before, 1, 0)).astype(jnp.int32)
        chosen = (peer_col == peer) & (rank == place)
        target = down(jnp.where(chosen, line, 0)).astype(jnp.int32) - 1
        total_u = jnp.zeros((rows, MSG), F32)
        total_d = jnp.zeros((rows, MSG), F32)
        for start in range(0, columns, chunk):
            here = lax.broadcasted_iota(jnp.int32, (chunk, MSG), 0) + start
            pick = jnp.where(here == target, 1.0, 0.0).astype(BF16)
            total_u += dot(u_ref[:, start : start + chunk], pick)
            total_d += dot(d_ref[:, start : start + chunk], pick)
        out[peer, 0:rows, :] = total_u.astype(BF16)
        out[peer, rows : 2 * rows, :] = total_d.astype(BF16)
        degrees = down(jnp.where(chosen, degree, 0.0))
        out[peer, 2 * rows :, :] = jnp.broadcast_to(degrees, (16, MSG)).astype(BF16)


def penalty_kernel(
    parts,
    block_elements,
    me_ref,
    u_in,
    d_in,
    row_ref,
    col_ref,
    deg_ref,
    degt_ref,
    weight_ref,
    mass_ref,
    near_in,
    out_u,
    out_d,
    others,
    u_ref,
    d_ref,
    sem,
    near,
    near_sem,
):
    me = me_ref[0]
    near_copies = [
        fetch(near_in.at[lax.rem(me + offset + parts, parts)], near.at[i], near_sem.at[i])
        for i, offset in enumerate(OFFSETS)
    ]
    copies = [fetch(u_in, u_ref, sem.at[0]), fetch(d_in, d_ref, sem.at[1])]
    for copy in near_copies + copies:
        copy.start()
    rows, columns = u_ref.shape
    side_col, flag_col, peer_col, slot_col = (col_ref[:, i : i + 1] for i in range(4))
    side_row, peer_row, slot_row = row_ref[0:1, :], row_ref[2:3, :], row_ref[3:4, :]
    slots = side_col.shape[0]
    nodes = slots * NQ
    base_col, step_col = slot_line(side_col, block_elements)
    base_row, step_row = slot_line(side_row, block_elements)
    degree_col = degree_column(side_col, deg_ref[...])
    elements = degt_ref.shape[0]
    level = lax.broadcasted_iota(jnp.int32, (elements, slots), 0)
    mine = level == lax.shift_right_logical(side_row, 2)
    value = jnp.where(jnp.bitwise_and(side_row, 1) == 0, degt_ref[:, 0:1], degt_ref[:, 1:2])
    degree_row = down(jnp.where(mine, value, 0))

    lane_slot = lax.broadcasted_iota(jnp.int32, (slots, slots), 1)
    partner = lane_slot == slot_col
    partner_base = across(jnp.where(partner, base_row, 0)).astype(jnp.int32)
    partner_step = across(jnp.where(partner, step_row, 0)).astype(jnp.int32)
    inner_degree = across(jnp.where(partner, degree_row, 0.0))
    rank = across(jnp.where((peer_row == peer_col) & (slot_row < slot_col), 1, 0)).astype(
        jnp.int32
    )
    for copy in near_copies:
        copy.wait()
    source = partner_base
    source_step = partner_step
    other_degree = inner_degree
    lane_msg = lax.broadcasted_iota(jnp.int32, (slots, MSG), 1)
    at_rank = lane_msg == rank * NQ
    for index, offset in enumerate(OFFSETS):
        from_here = peer_col == lax.rem(me + offset + parts, parts)
        far_degree = near[index, 2 * rows : 2 * rows + 16, :].astype(F32)[0:1, :]
        source = jnp.where(from_here, columns + index * MSG + rank * NQ, source)
        source_step = jnp.where(from_here, 1, source_step)
        other_degree = jnp.where(
            from_here, across(jnp.where(at_rank, far_degree, 0.0)), other_degree
        )
    live = peer_col >= 0
    turned = flag_col == 1
    source = jnp.where(turned, source + 7 * source_step, source)
    source_step = jnp.where(turned, -source_step, source_step)
    source = jnp.where(live, source, -1)
    source_step = jnp.where(live, source_step, 0)
    joint = jnp.maximum(degree_col, other_degree) + 1.0
    strength = jnp.where(live, PENALTY * joint * joint, 0.0)

    lane = lax.broadcasted_iota(jnp.int32, (slots, nodes), 1)
    owner = lax.shift_right_logical(lane, 3) == lax.broadcasted_iota(jnp.int32, (slots, nodes), 0)
    node = jnp.bitwise_and(lane, 7)
    own_line = down(jnp.where(owner, base_col + step_col * node, 0)).astype(jnp.int32)
    far_line = down(jnp.where(owner, source + source_step * node, 0)).astype(jnp.int32)
    factor = down(jnp.where(owner, strength, 0.0)) * weight_ref[...]
    factor_high = factor.astype(BF16).astype(F32)
    factor_low = factor - factor_high

    chunk = min(512, columns)
    for copy in copies:
        copy.wait()
    total_u = jnp.zeros((rows, nodes), F32)
    total_d = jnp.zeros((rows, nodes), F32)
    for start in range(0, columns, chunk):
        here = lax.broadcasted_iota(jnp.int32, (chunk, nodes), 0) + start
        pick = jnp.where(here == far_line, 1.0, 0.0).astype(BF16)
        total_u += dot(u_ref[:, start : start + chunk], pick)
        total_d += dot(d_ref[:, start : start + chunk], pick)
    for index in range(len(OFFSETS)):
        here = lax.broadcasted_iota(jnp.int32, (MSG, nodes), 0) + (columns + index * MSG)
        pick = jnp.where(here == far_line, 1.0, 0.0).astype(BF16)
        total_u += dot(near[index, 0:rows, :], pick)
        total_d += dot(near[index, rows : 2 * rows, :], pick)
    others[0:rows, :] = total_u.astype(BF16)
    others[rows : 2 * rows, :] = total_d.astype(BF16)
    others[2 * rows :, :] = jnp.ones((16, nodes), BF16)

    for start in range(0, columns, chunk):
        here = lax.broadcasted_iota(jnp.int32, (chunk, nodes), 0) + start
        match = here == own_line
        spread_high = jnp.where(match, factor_high, 0.0).astype(BF16)
        spread_low = jnp.where(match, factor_low, 0.0).astype(BF16)
        pulled = lax.dot_general(
            others[...], spread_high, NT, preferred_element_type=F32
        ) + lax.dot_general(others[...], spread_low, NT, preferred_element_type=F32)
        at = slice(start, start + chunk)
        scale = HELM_LAMBDA * mass_ref[:, at] + pulled[2 * rows : 2 * rows + 1, :]
        out_u[:, at] = scale * u_ref[:, at].astype(F32) - pulled[0:rows, :]
        out_d[:, at] = scale * d_ref[:, at].astype(F32) - pulled[rows : 2 * rows, :]


def finish_kernel(near, width, with_local, me_ref, *refs):
    fields = len(with_local)
    count = sum(with_local)
    pieces, refs = refs[: len(near)], refs[len(near) :]
    locals_in, outs = refs[:count], refs[-fields - 2 : -2]
    result, sem = refs[-2:]
    me = me_ref[0]
    stores = []
    for n, d in enumerate(near):
        at = pl.ds(pl.multiple_of(jnp.bitwise_xor(me, d) * width, width), width)
        seen = 0
        for f in range(fields):
            value = pieces[n][f].astype(F32)
            if with_local[f]:
                value = value + locals_in[seen][:, at]
                seen += 1
            result[f, n] = value
            stores.append(pltpu.make_async_copy(result.at[f, n], outs[f].at[:, at], sem.at[f, n]))
            stores[-1].start()
    for store in stores:
        store.wait()


def finish(pieces, near, local, me, begun=None):
    modes = len(pieces)
    fields, rows, width = pieces[0].shape
    with_local = tuple(part is not None for part in local)
    present = [part for part in local if part is not None]
    operands = [me, *[pieces[d] for d in near], *present, *(begun or [])]
    anywhere = pl.BlockSpec(memory_space=pl.ANY)
    begin = len(operands) - fields
    return pl.pallas_call(
        functools.partial(finish_kernel, tuple(near), width, with_local),
        out_shape=[jax.ShapeDtypeStruct((rows, modes * width), F32)] * fields,
        in_specs=[SMEM]
        + [VMEM] * (len(near) + len(present))
        + [anywhere] * (fields if begun else 0),
        out_specs=[anywhere] * fields,
        input_output_aliases={begin + f: f for f in range(fields)} if begun else {},
        scratch_shapes=[
            pltpu.VMEM((fields, len(near), rows, width), F32),
            pltpu.SemaphoreType.DMA((fields, len(near))),
        ],
        compiler_params=pltpu.CompilerParams(vmem_limit_bytes=16 * MIB),
        name="finish_rest" if begun else "finish",
    )(*operands)


def swap_with(block, axis, distance):
    count = lax.axis_size(axis)
    return lax.ppermute(block, axis, [(i, i ^ distance) for i in range(count)])


def on_device(u_spec, dir_spec, advecting, viscosity, degrees, edge_side, edge_link):
    modes = lax.axis_size("mode")
    parts = lax.axis_size("elem")
    total, width = viscosity.shape
    rows, columns = u_spec.shape
    block_elements = degrees.shape[1] // modes
    slots = edge_side.shape[0]
    my_mode = lax.axis_index("mode")
    mode_id = my_mode.astype(jnp.int32).reshape(1)
    part_id = lax.axis_index("elem").astype(jnp.int32).reshape(1)

    derivative, weights = cheb_tables()
    identity = np.eye(block_elements)
    kron_x = np.kron(METRIC * derivative, np.eye(NQ * block_elements))
    group = width
    if width % 256 == 0 and 256 % (NQ * block_elements) == 0:
        group = 256
    kron_y = np.kron(np.eye(group // (NQ * block_elements)), np.kron(METRIC * derivative, identity))
    mass = np.repeat(AREA_SCALE * np.outer(weights, weights).reshape(-1), block_elements)
    synthesis, sloped = synthesis_tables(total)
    tables = [
        jnp.asarray(t)
        for t in (
            synthesis,
            sloped,
            np.ascontiguousarray(synthesis.T),
            np.ascontiguousarray(sloped.T),
            split_pair(kron_x.T),
            split_pair(kron_y.T),
            split_pair(kron_x),
            split_pair(kron_y),
        )
    ]
    mass_row = jnp.asarray(mass.astype(np.float32)[None, :])

    def cut(field):
        return pl.pallas_call(
            functools.partial(cut_kernel, modes),
            out_shape=[jax.ShapeDtypeStruct((rows, width), BF16)] * (modes - 1),
            in_specs=[SMEM, pl.BlockSpec(memory_space=pltpu.HBM)],
            out_specs=[VMEM] * (modes - 1),
            scratch_shapes=[pltpu.SemaphoreType.DMA((modes - 1,))],
            compiler_params=pltpu.CompilerParams(vmem_limit_bytes=8 * MIB),
            name="cut",
        )(mode_id, field)

    order = [*range(2, modes), 1]
    u_cut = cut(u_spec)
    far = pl.BlockSpec(memory_space=pltpu.HBM)
    fields_held = [pltpu.VMEM((rows, columns), BF16)] * 2 + [pltpu.SemaphoreType.DMA((2,))]
    edge_side, edge_link, u_cut = lax.optimization_barrier((edge_side, edge_link, u_cut))
    table_row = jnp.concatenate([edge_side[None, :], edge_link], axis=0)
    table_col = table_row.T
    messages = pl.pallas_call(
        functools.partial(traces_kernel, parts, block_elements),
        out_shape=jax.ShapeDtypeStruct((parts, 2 * rows + 16, MSG), BF16),
        in_specs=[SMEM, far, far] + [VMEM] * 3,
        out_specs=VMEM,
        scratch_shapes=fields_held,
        compiler_params=pltpu.CompilerParams(vmem_limit_bytes=20 * MIB),
        name="traces",
    )(part_id, u_spec, dir_spec, table_row, table_col, degrees)

    u_pieces = [u_spec] + [None] * (modes - 1)
    for d in order:
        u_pieces[d] = swap_with(u_cut[d - 1], "mode", d)
    d_cut, u_pieces[1] = lax.optimization_barrier((cut(dir_spec), u_pieces[1]))
    d_pieces = [dir_spec] + [None] * (modes - 1)
    for d in order:
        d_pieces[d] = swap_with(d_cut[d - 1], "mode", d)

    u_pieces[1], messages = lax.optimization_barrier((u_pieces[1], messages))
    near = lax.all_to_all(messages, "elem", split_axis=0, concat_axis=0, tiled=True)
    u_back = planes(u_pieces, tables, viscosity, mass_row, advecting, mode_id)
    d_pieces[1], u_back = lax.optimization_barrier((d_pieces[1], list(u_back)))
    u_returned = [u_back[0]] + [None] * (modes - 1)
    for d in order:
        u_returned[d] = swap_with(u_back[d], "mode", d)
    d_back = planes(d_pieces, tables, viscosity, mass_row, None, mode_id)

    edge_weight = np.tile(LENGTH * weights, slots).astype(np.float32)[None, :]
    mass_local = np.tile(mass, modes).astype(np.float32)[None, :]
    local_u, local_d = pl.pallas_call(
        functools.partial(penalty_kernel, parts, block_elements),
        out_shape=[jax.ShapeDtypeStruct((rows, columns), F32)] * 2,
        in_specs=[SMEM, far, far] + [VMEM] * 6 + [far],
        out_specs=[VMEM] * 2,
        scratch_shapes=[pltpu.VMEM((2 * rows + 16, slots * NQ), BF16)]
        + fields_held
        + [
            pltpu.VMEM((len(OFFSETS), 2 * rows + 16, MSG), BF16),
            pltpu.SemaphoreType.DMA((len(OFFSETS),)),
        ],
        compiler_params=pltpu.CompilerParams(vmem_limit_bytes=32 * MIB),
        cost_estimate=pl.CostEstimate(
            flops=2 * 2 * rows * slots * NQ * 3 * columns,
            bytes_accessed=20 * rows * columns,
            transcendentals=0,
        ),
        name="penalty",
    )(
        part_id,
        u_spec,
        dir_spec,
        table_row,
        table_col,
        degrees,
        degrees.T,
        jnp.asarray(edge_weight),
        jnp.asarray(mass_local),
        near,
    )

    d_back, u_returned[1], local_d = lax.optimization_barrier((d_back, u_returned[1], local_d))
    d_returned = [d_back[0]] + [None] * (modes - 1)
    for d in order:
        d_returned[d] = swap_with(d_back[d], "mode", d)
    advect, helm_velocity = finish(u_returned, range(modes), [None, local_u], mode_id)
    begun = finish(d_returned, [0], [local_d], mode_id)
    (helm_direction,) = finish(d_returned, range(1, modes), [local_d], mode_id, list(begun))
    return (advect, helm_velocity, helm_direction)


def solution(mesh):
    in_specs = (
        P("mode", "elem"),
        P("mode", "elem"),
        P(None, None, ("elem", "mode")),
        P(None, ("elem", "mode")),
        P(None, "elem"),
        P("elem"),
        P(None, "elem"),
    )
    out_specs = (P("mode", "elem"), P("mode", "elem"), P("mode", "elem"))
    return jax.shard_map(
        on_device, mesh=mesh, in_specs=in_specs, out_specs=out_specs, check_vma=False
    )
```

```python
import functools
import math

import jax
import jax.numpy as jnp
import ml_dtypes
import numpy as np
from jax import lax
from jax.experimental import pallas as pl
from jax.experimental.pallas import tpu as pltpu
from jax.sharding import PartitionSpec as P

NQ = 8
METRIC = 0.125
AREA_SCALE = 64.0
LENGTH = 8.0
HELM_LAMBDA = 4.0
PENALTY = 0.02
OFFSETS = (1, 2, -1, -2)
MSG = 256
MIB = 1024 * 1024
PLANES_LIMIT = 56

F32 = jnp.float32
BF16 = jnp.bfloat16
VMEM = pl.BlockSpec(memory_space=pltpu.VMEM)
SMEM = pl.BlockSpec(memory_space=pltpu.SMEM)
NT = (((1,), (1,)), ((), ()))


def cheb_tables():
    degree_top = 7
    angles = np.pi * np.arange(degree_top + 1) / degree_top
    cheb_points = np.cos(angles)
    signs_scale = np.ones(degree_top + 1)
    signs_scale[0] = 2.0
    signs_scale[degree_top] = 2.0
    signs_scale = signs_scale * (-1.0) ** np.arange(degree_top + 1)
    differences = cheb_points[:, None] - cheb_points[None, :]
    derivative = (
        signs_scale[:, None] / signs_scale[None, :] / (differences + np.eye(degree_top + 1))
    )
    derivative = derivative - np.eye(degree_top + 1) * derivative.sum(axis=1)[:, None]
    weights = np.zeros(degree_top + 1)
    interior = np.ones(degree_top - 1)
    for k in range(1, (degree_top - 1) // 2 + 1):
        interior = interior - 2.0 * np.cos(2 * k * angles[1:degree_top]) / (4 * k * k - 1)
    weights[0] = 1.0 / (degree_top * degree_top)
    weights[degree_top] = weights[0]
    weights[1:degree_top] = 2.0 * interior / degree_top
    return (derivative, weights)


def split_pair(matrix):
    matrix = matrix.astype(np.float32)
    high = matrix.astype(ml_dtypes.bfloat16)
    low = (matrix - high.astype(np.float32)).astype(ml_dtypes.bfloat16)
    return np.concatenate([high, high, low], axis=0)


def synthesis_tables(total):
    planes = np.arange(total)
    turn = (planes[:, None] * (planes // 2)[None, :]) % total
    angles = np.float32(2.0 * math.pi / total) * turn.astype(np.float32)
    angles = angles.astype(np.float64)
    table = np.where(planes[None, :] % 2 == 0, np.cos(angles), np.sin(angles))
    table = table * math.sqrt(2.0 / total)
    table[:, 0] = 1.0 / math.sqrt(total)
    table[:, 1] = (1 - 2 * (planes % 2)) / math.sqrt(total)
    rounded = table.astype(np.float32).astype(ml_dtypes.bfloat16)
    exact = rounded.astype(np.float64)
    rate = 4.0 / total * (planes[::2] // 2)
    sloped = np.zeros_like(exact)
    sloped[:, 1::2] = exact[:, 0::2] * rate[None, :]
    sloped[:, 0::2] = -exact[:, 1::2] * rate[None, :]
    return rounded, sloped.astype(np.float32).astype(ml_dtypes.bfloat16)


def shift_of(number):
    assert number & (number - 1) == 0
    return number.bit_length() - 1


def dot(a, b):
    return jnp.dot(a, b, preferred_element_type=F32)


def dot_split(value, table):
    high = value.astype(BF16)
    low = (value - high.astype(F32)).astype(BF16)
    return dot(jnp.concatenate([high, low, high], axis=1), table)


def cut_kernel(modes, me_ref, field, *refs):
    pieces, sem = refs[:-1], refs[-1]
    me = me_ref[0]
    width = pieces[0].shape[1]
    copies = []
    for d in range(1, modes):
        at = pl.ds(pl.multiple_of(jnp.bitwise_xor(me, d) * width, width), width)
        copies.append(pltpu.make_async_copy(field.at[:, at], pieces[d - 1], sem.at[d - 1]))
        copies[-1].start()
    for copy in copies:
        copy.wait()


def planes_kernel(modes, chunk, advected, me_ref, *refs):
    own_ref, pieces = refs[0], refs[1:modes]
    s_in, sz_in, t_in, tz_in, *node_in = refs[modes : modes + 8]
    visc_in, mass_ref = refs[modes + 8 : modes + 10]
    refs = refs[modes + 10 :]
    if advected:
        adv_in, refs = refs[0], refs[1:]
    outs = refs[:modes]
    spec, flat, flux, s_ref, sz_ref, t_ref, tz_ref, visc_ref = refs[modes : modes + 8]
    rx_ref, ry_ref, kx_ref, ky_ref = node_refs = refs[modes + 8 : modes + 12]
    held, step_sem, node_sem, own_sem, back_sem, out_sem = refs[modes + 12 : modes + 18]
    if advected:
        moved, adv_ref = refs[modes + 18 :]
    me = me_ref[0]
    rows = own_ref.shape[0]
    total, width = visc_ref.shape
    group = ry_ref.shape[1]
    steps = total // chunk

    own_copy = pltpu.make_async_copy(
        own_ref.at[:, pl.ds(pl.multiple_of(me * width, width), width)],
        spec.at[pl.ds(pl.multiple_of(me * rows, rows), rows), :],
        own_sem,
    )
    node_copies = [
        pltpu.make_async_copy(source, target, node_sem.at[i])
        for i, (source, target) in enumerate(zip(node_in, node_refs))
    ]
    back_copies = [
        pltpu.make_async_copy(t_in, t_ref, back_sem.at[0]),
        pltpu.make_async_copy(tz_in, tz_ref, back_sem.at[1]),
    ]

    def plane_copies(step):
        at = pl.ds(pl.multiple_of(step * chunk, chunk), chunk)
        pairs = [(s_in, s_ref), (sz_in, sz_ref), (visc_in, visc_ref)]
        copies = [
            pltpu.make_async_copy(source.at[at, :], target.at[at, :], step_sem.at[step, i])
            for i, (source, target) in enumerate(pairs)
        ]
        if advected:
            copies.append(
                pltpu.make_async_copy(
                    adv_in.at[:, at, :], adv_ref.at[:, at, :], step_sem.at[step, 3]
                )
            )
        return copies

    own_copy.start()
    first = plane_copies(0)
    for copy in first[:2] + node_copies[:2] + first[2:] + node_copies[2:]:
        copy.start()
    for step in range(1, steps):
        for copy in plane_copies(step):
            copy.start()
    for copy in back_copies:
        copy.start()
    for d in range(1, modes):
        at = pl.ds(pl.multiple_of(jnp.bitwise_xor(me, d) * rows, rows), rows)
        spec[at, :] = pieces[d - 1][...]
    own_copy.wait()

    def grouped(value, ref):
        parts = [
            dot_split(value[:, g : g + group], ref[...]) for g in range(0, width, group)
        ]
        return parts[0] if len(parts) == 1 else jnp.concatenate(parts, axis=1)

    def forward(step, carry):
        at = pl.ds(pl.multiple_of(step * chunk, chunk), chunk)
        copies = plane_copies(step)
        for copy in copies[:2]:
            copy.wait()
        coeffs = spec[...]
        plain = dot(s_ref[at, :], coeffs)
        along = dot(sz_ref[at, :], coeffs)

        @pl.when(step == 0)
        def _():
            for copy in node_copies:
                copy.wait()

        for copy in copies[2:]:
            copy.wait()
        grad_x = dot_split(plain, rx_ref[...])
        grad_y = grouped(plain, ry_ref)
        weighted = mass_ref[...] * visc_ref[at, :].astype(F32)
        if advected:
            moved[at, :] = (
                adv_ref[0, at, :].astype(F32) * grad_x
                + adv_ref[1, at, :].astype(F32) * grad_y
                + adv_ref[2, at, :].astype(F32) * along
            ).astype(BF16)
        flux[at, :] = (weighted * along).astype(BF16)
        flat_sum = dot_split(weighted * grad_x, kx_ref[...]) + grouped(weighted * grad_y, ky_ref)
        flat[at, :] = flat_sum.astype(BF16)
        return carry

    lax.fori_loop(0, steps, forward, 0)

    for copy in back_copies:
        copy.wait()
    stores = [pltpu.make_async_copy(held.at[d], outs[d], out_sem.at[d]) for d in range(modes)]
    for d in [*range(1, modes), 0]:
        at = pl.ds(pl.multiple_of(jnp.bitwise_xor(me, d) * rows, rows), rows)
        volume = dot(t_ref[at, :], flat[...]) + dot(tz_ref[at, :], flux[...])
        if advected:
            held[d, 0] = dot(t_ref[at, :], moved[...]).astype(BF16)
            held[d, 1] = volume.astype(BF16)
        else:
            held[d, 0] = volume.astype(BF16)
        stores[d].start()
    for store in stores:
        store.wait()


def planes(pieces, tables, visc, mass, adv, me):
    modes = len(pieces)
    rows = pieces[0].shape[0]
    total, width = visc.shape
    group = tables[5].shape[1]
    chunk = min(256, total)
    advected = adv is not None
    fields = 2 if advected else 1
    operands = [me, *pieces, *tables, visc, mass] + ([adv] if advected else [])
    flops = 2 * total * total * width * (2 + 2 + (1 if advected else 0))
    flops += 2 * total * width * width * 9
    far = pl.BlockSpec(memory_space=pltpu.HBM)
    plane = pltpu.VMEM((total, width), BF16)
    square = pltpu.VMEM((total, total), BF16)
    node_x = pltpu.VMEM((3 * width, width), BF16)
    node_y = pltpu.VMEM((3 * group, group), BF16)
    scratch = [plane] * 3 + [square] * 4 + [plane, node_x, node_y, node_x, node_y]
    scratch += [
        pltpu.VMEM((modes, fields, rows, width), BF16),
        pltpu.SemaphoreType.DMA((total // chunk, 4)),
        pltpu.SemaphoreType.DMA((4,)),
        pltpu.SemaphoreType.DMA,
        pltpu.SemaphoreType.DMA((2,)),
        pltpu.SemaphoreType.DMA((modes,)),
    ]
    if advected:
        scratch += [plane, pltpu.VMEM(adv.shape, BF16)]
    return pl.pallas_call(
        functools.partial(planes_kernel, modes, chunk, advected),
        out_shape=[jax.ShapeDtypeStruct((fields, rows, width), BF16)] * modes,
        in_specs=[SMEM, far]
        + [VMEM] * (modes - 1)
        + [far] * (len(tables) + 1)
        + [VMEM]
        + [far] * (1 if advected else 0),
        out_specs=[far] * modes,
        scratch_shapes=scratch,
        compiler_params=pltpu.CompilerParams(vmem_limit_bytes=PLANES_LIMIT * MIB),
        cost_estimate=pl.CostEstimate(
            flops=flops, bytes_accessed=12 * total * total, transcendentals=0
        ),
        name="planes_moved" if advected else "planes_plain",
    )(*operands)


def slot_line(side, block_elements):
    element = lax.shift_right_logical(side, 2)
    code = jnp.bitwise_and(side, 3)
    first = jnp.where(code == 0, 0, jnp.where(code == 1, 7, jnp.where(code == 2, 63, 56)))
    step = jnp.where(code == 0, 1, jnp.where(code == 1, 8, jnp.where(code == 2, -1, -8)))
    block = lax.shift_right_logical(element, shift_of(block_elements))
    inner = jnp.bitwise_and(element, block_elements - 1)
    base = block * (NQ * NQ * block_elements) + first * block_elements + inner
    return base, step * block_elements


def across(values):
    return jnp.sum(values.astype(F32), axis=1, keepdims=True)


def down(values):
    return jnp.sum(values.astype(F32), axis=0, keepdims=True)


def degree_column(side_col, degrees):
    slots = side_col.shape[0]
    elements = degrees.shape[1]
    lanes = lax.broadcasted_iota(jnp.int32, (slots, elements), 1)
    mine = lanes == lax.shift_right_logical(side_col, 2)
    along_x = jnp.bitwise_and(side_col, 1) == 0
    value = jnp.where(along_x, degrees[0:1, :], degrees[1:2, :])
    return across(jnp.where(mine, value, 0))


def fetch(source, target, sem):
    return pltpu.make_async_copy(source, target, sem)


def traces_kernel(parts, block_elements, me_ref, u_in, d_in, row_ref, col_ref, deg_ref, *refs):
    out, u_ref, d_ref, sem = refs
    copies = [fetch(u_in, u_ref, sem.at[0]), fetch(d_in, d_ref, sem.at[1])]
    for copy in copies:
        copy.start()
    me = me_ref[0]
    rows, columns = u_ref.shape
    side_col = col_ref[:, 0:1]
    peer_col = col_ref[:, 2:3]
    peer_row = row_ref[2:3, :]
    slots = side_col.shape[0]
    base, step = slot_line(side_col, block_elements)
    degree = degree_column(side_col, deg_ref[...])
    before = lax.broadcasted_iota(jnp.int32, (slots, slots), 1) < lax.broadcasted_iota(
        jnp.int32, (slots, slots), 0
    )
    lane = lax.broadcasted_iota(jnp.int32, (slots, MSG), 1)
    place = lax.shift_right_logical(lane, 3)
    line = base + step * jnp.bitwise_and(lane, 7) + 1
    chunk = min(512, columns)
    for copy in copies:
        copy.wait()
    for offset in OFFSETS:
        peer = lax.rem(me + offset + parts, parts)
        rank = across(jnp.where((peer_row == peer) & before, 1, 0)).astype(jnp.int32)
        chosen = (peer_col == peer) & (rank == place)
        target = down(jnp.where(chosen, line, 0)).astype(jnp.int32) - 1
        total_u = jnp.zeros((rows, MSG), F32)
        total_d = jnp.zeros((rows, MSG), F32)
        for start in range(0, columns, chunk):
            here = lax.broadcasted_iota(jnp.int32, (chunk, MSG), 0) + start
            pick = jnp.where(here == target, 1.0, 0.0).astype(BF16)
            total_u += dot(u_ref[:, start : start + chunk], pick)
            total_d += dot(d_ref[:, start : start + chunk], pick)
        out[peer, 0:rows, :] = total_u.astype(BF16)
        out[peer, rows : 2 * rows, :] = total_d.astype(BF16)
        degrees = down(jnp.where(chosen, degree, 0.0))
        out[peer, 2 * rows :, :] = jnp.broadcast_to(degrees, (16, MSG)).astype(BF16)


def penalty_kernel(
    parts,
    block_elements,
    me_ref,
    u_in,
    d_in,
    row_ref,
    col_ref,
    deg_ref,
    degt_ref,
    weight_ref,
    mass_ref,
    near_in,
    out_u,
    out_d,
    others,
    u_ref,
    d_ref,
    sem,
    near,
    near_sem,
):
    me = me_ref[0]
    near_copies = [
        fetch(near_in.at[lax.rem(me + offset + parts, parts)], near.at[i], near_sem.at[i])
        for i, offset in enumerate(OFFSETS)
    ]
    copies = [fetch(u_in, u_ref, sem.at[0]), fetch(d_in, d_ref, sem.at[1])]
    for copy in near_copies + copies:
        copy.start()
    rows, columns = u_ref.shape
    side_col, flag_col, peer_col, slot_col = (col_ref[:, i : i + 1] for i in range(4))
    side_row, peer_row, slot_row = row_ref[0:1, :], row_ref[2:3, :], row_ref[3:4, :]
    slots = side_col.shape[0]
    nodes = slots * NQ
    base_col, step_col = slot_line(side_col, block_elements)
    base_row, step_row = slot_line(side_row, block_elements)
    degree_col = degree_column(side_col, deg_ref[...])
    elements = degt_ref.shape[0]
    level = lax.broadcasted_iota(jnp.int32, (elements, slots), 0)
    mine = level == lax.shift_right_logical(side_row, 2)
    value = jnp.where(jnp.bitwise_and(side_row, 1) == 0, degt_ref[:, 0:1], degt_ref[:, 1:2])
    degree_row = down(jnp.where(mine, value, 0))

    lane_slot = lax.broadcasted_iota(jnp.int32, (slots, slots), 1)
    partner = lane_slot == slot_col
    partner_base = across(jnp.where(partner, base_row, 0)).astype(jnp.int32)
    partner_step = across(jnp.where(partner, step_row, 0)).astype(jnp.int32)
    inner_degree = across(jnp.where(partner, degree_row, 0.0))
    rank = across(jnp.where((peer_row == peer_col) & (slot_row < slot_col), 1, 0)).astype(
        jnp.int32
    )
    for copy in near_copies:
        copy.wait()
    source = partner_base
    source_step = partner_step
    other_degree = inner_degree
    lane_msg = lax.broadcasted_iota(jnp.int32, (slots, MSG), 1)
    at_rank = lane_msg == rank * NQ
    for index, offset in enumerate(OFFSETS):
        from_here = peer_col == lax.rem(me + offset + parts, parts)
        far_degree = near[index, 2 * rows : 2 * rows + 16, :].astype(F32)[0:1, :]
        source = jnp.where(from_here, columns + index * MSG + rank * NQ, source)
        source_step = jnp.where(from_here, 1, source_step)
        other_degree = jnp.where(
            from_here, across(jnp.where(at_rank, far_degree, 0.0)), other_degree
        )
    live = peer_col >= 0
    turned = flag_col == 1
    source = jnp.where(turned, source + 7 * source_step, source)
    source_step = jnp.where(turned, -source_step, source_step)
    source = jnp.where(live, source, -1)
    source_step = jnp.where(live, source_step, 0)
    joint = jnp.maximum(degree_col, other_degree) + 1.0
    strength = jnp.where(live, PENALTY * joint * joint, 0.0)

    lane = lax.broadcasted_iota(jnp.int32, (slots, nodes), 1)
    owner = lax.shift_right_logical(lane, 3) == lax.broadcasted_iota(jnp.int32, (slots, nodes), 0)
    node = jnp.bitwise_and(lane, 7)
    own_line = down(jnp.where(owner, base_col + step_col * node, 0)).astype(jnp.int32)
    far_line = down(jnp.where(owner, source + source_step * node, 0)).astype(jnp.int32)
    factor = down(jnp.where(owner, strength, 0.0)) * weight_ref[...]
    factor_high = factor.astype(BF16).astype(F32)
    factor_low = factor - factor_high

    chunk = min(512, columns)
    for copy in copies:
        copy.wait()
    total_u = jnp.zeros((rows, nodes), F32)
    total_d = jnp.zeros((rows, nodes), F32)
    for start in range(0, columns, chunk):
        here = lax.broadcasted_iota(jnp.int32, (chunk, nodes), 0) + start
        pick = jnp.where(here == far_line, 1.0, 0.0).astype(BF16)
        total_u += dot(u_ref[:, start : start + chunk], pick)
        total_d += dot(d_ref[:, start : start + chunk], pick)
    for index in range(len(OFFSETS)):
        here = lax.broadcasted_iota(jnp.int32, (MSG, nodes), 0) + (columns + index * MSG)
        pick = jnp.where(here == far_line, 1.0, 0.0).astype(BF16)
        total_u += dot(near[index, 0:rows, :], pick)
        total_d += dot(near[index, rows : 2 * rows, :], pick)
    others[0:rows, :] = total_u.astype(BF16)
    others[rows : 2 * rows, :] = total_d.astype(BF16)
    others[2 * rows :, :] = jnp.ones((16, nodes), BF16)

    for start in range(0, columns, chunk):
        here = lax.broadcasted_iota(jnp.int32, (chunk, nodes), 0) + start
        match = here == own_line
        spread_high = jnp.where(match, factor_high, 0.0).astype(BF16)
        spread_low = jnp.where(match, factor_low, 0.0).astype(BF16)
        pulled = lax.dot_general(
            others[...], spread_high, NT, preferred_element_type=F32
        ) + lax.dot_general(others[...], spread_low, NT, preferred_element_type=F32)
        at = slice(start, start + chunk)
        scale = HELM_LAMBDA * mass_ref[:, at] + pulled[2 * rows : 2 * rows + 1, :]
        out_u[:, at] = scale * u_ref[:, at].astype(F32) - pulled[0:rows, :]
        out_d[:, at] = scale * d_ref[:, at].astype(F32) - pulled[rows : 2 * rows, :]


def finish_kernel(near, width, with_local, me_ref, *refs):
    fields = len(with_local)
    count = sum(with_local)
    pieces, refs = refs[: len(near)], refs[len(near) :]
    locals_in, outs = refs[:count], refs[-fields - 2 : -2]
    result, sem = refs[-2:]
    me = me_ref[0]
    stores = []
    for n, d in enumerate(near):
        at = pl.ds(pl.multiple_of(jnp.bitwise_xor(me, d) * width, width), width)
        seen = 0
        for f in range(fields):
            value = pieces[n][f].astype(F32)
            if with_local[f]:
                value = value + locals_in[seen][:, at]
                seen += 1
            result[f, n] = value
            stores.append(pltpu.make_async_copy(result.at[f, n], outs[f].at[:, at], sem.at[f, n]))
            stores[-1].start()
    for store in stores:
        store.wait()


def finish(pieces, near, local, me, begun=None):
    modes = len(pieces)
    fields, rows, width = pieces[0].shape
    with_local = tuple(part is not None for part in local)
    present = [part for part in local if part is not None]
    operands = [me, *[pieces[d] for d in near], *present, *(begun or [])]
    anywhere = pl.BlockSpec(memory_space=pl.ANY)
    begin = len(operands) - fields
    return pl.pallas_call(
        functools.partial(finish_kernel, tuple(near), width, with_local),
        out_shape=[jax.ShapeDtypeStruct((rows, modes * width), F32)] * fields,
        in_specs=[SMEM]
        + [VMEM] * (len(near) + len(present))
        + [anywhere] * (fields if begun else 0),
        out_specs=[anywhere] * fields,
        input_output_aliases={begin + f: f for f in range(fields)} if begun else {},
        scratch_shapes=[
            pltpu.VMEM((fields, len(near), rows, width), F32),
            pltpu.SemaphoreType.DMA((fields, len(near))),
        ],
        compiler_params=pltpu.CompilerParams(vmem_limit_bytes=16 * MIB),
        name="finish_rest" if begun else "finish",
    )(*operands)


def swap_with(block, axis, distance):
    count = lax.axis_size(axis)
    return lax.ppermute(block, axis, [(i, i ^ distance) for i in range(count)])


def on_device(u_spec, dir_spec, advecting, viscosity, degrees, edge_side, edge_link):
    modes = lax.axis_size("mode")
    parts = lax.axis_size("elem")
    total, width = viscosity.shape
    rows, columns = u_spec.shape
    block_elements = degrees.shape[1] // modes
    slots = edge_side.shape[0]
    my_mode = lax.axis_index("mode")
    mode_id = my_mode.astype(jnp.int32).reshape(1)
    part_id = lax.axis_index("elem").astype(jnp.int32).reshape(1)

    derivative, weights = cheb_tables()
    identity = np.eye(block_elements)
    kron_x = np.kron(METRIC * derivative, np.eye(NQ * block_elements))
    group = width
    if width % 256 == 0 and 256 % (NQ * block_elements) == 0:
        group = 256
    kron_y = np.kron(np.eye(group // (NQ * block_elements)), np.kron(METRIC * derivative, identity))
    mass = np.repeat(AREA_SCALE * np.outer(weights, weights).reshape(-1), block_elements)
    synthesis, sloped = synthesis_tables(total)
    tables = [
        jnp.asarray(t)
        for t in (
            synthesis,
            sloped,
            np.ascontiguousarray(synthesis.T),
            np.ascontiguousarray(sloped.T),
            split_pair(kron_x.T),
            split_pair(kron_y.T),
            split_pair(kron_x),
            split_pair(kron_y),
        )
    ]
    mass_row = jnp.asarray(mass.astype(np.float32)[None, :])

    def cut(field):
        return pl.pallas_call(
            functools.partial(cut_kernel, modes),
            out_shape=[jax.ShapeDtypeStruct((rows, width), BF16)] * (modes - 1),
            in_specs=[SMEM, pl.BlockSpec(memory_space=pltpu.HBM)],
            out_specs=[VMEM] * (modes - 1),
            scratch_shapes=[pltpu.SemaphoreType.DMA((modes - 1,))],
            compiler_params=pltpu.CompilerParams(vmem_limit_bytes=8 * MIB),
            name="cut",
        )(mode_id, field)

    order = [*range(2, modes), 1]
    u_cut = cut(u_spec)
    far = pl.BlockSpec(memory_space=pltpu.HBM)
    fields_held = [pltpu.VMEM((rows, columns), BF16)] * 2 + [pltpu.SemaphoreType.DMA((2,))]
    edge_side, edge_link, u_cut = lax.optimization_barrier((edge_side, edge_link, u_cut))
    table_row = jnp.concatenate([edge_side[None, :], edge_link], axis=0)
    table_col = table_row.T
    messages = pl.pallas_call(
        functools.partial(traces_kernel, parts, block_elements),
        out_shape=jax.ShapeDtypeStruct((parts, 2 * rows + 16, MSG), BF16),
        in_specs=[SMEM, far, far] + [VMEM] * 3,
        out_specs=VMEM,
        scratch_shapes=fields_held,
        compiler_params=pltpu.CompilerParams(vmem_limit_bytes=20 * MIB),
        name="traces",
    )(part_id, u_spec, dir_spec, table_row, table_col, degrees)

    u_pieces = [u_spec] + [None] * (modes - 1)
    for d in order:
        u_pieces[d] = swap_with(u_cut[d - 1], "mode", d)
    d_cut, u_pieces[1] = lax.optimization_barrier((cut(dir_spec), u_pieces[1]))
    d_pieces = [dir_spec] + [None] * (modes - 1)
    for d in order:
        d_pieces[d] = swap_with(d_cut[d - 1], "mode", d)

    u_pieces[1], messages = lax.optimization_barrier((u_pieces[1], messages))
    near = lax.all_to_all(messages, "elem", split_axis=0, concat_axis=0, tiled=True)
    u_back = planes(u_pieces, tables, viscosity, mass_row, advecting, mode_id)
    d_pieces[1], u_back = lax.optimization_barrier((d_pieces[1], list(u_back)))
    u_returned = [u_back[0]] + [None] * (modes - 1)
    for d in order:
        u_returned[d] = swap_with(u_back[d], "mode", d)
    d_back = planes(d_pieces, tables, viscosity, mass_row, None, mode_id)

    edge_weight = np.tile(LENGTH * weights, slots).astype(np.float32)[None, :]
    mass_local = np.tile(mass, modes).astype(np.float32)[None, :]
    local_u, local_d = pl.pallas_call(
        functools.partial(penalty_kernel, parts, block_elements),
        out_shape=[jax.ShapeDtypeStruct((rows, columns), F32)] * 2,
        in_specs=[SMEM, far, far] + [VMEM] * 6 + [far],
        out_specs=[VMEM] * 2,
        scratch_shapes=[pltpu.VMEM((2 * rows + 16, slots * NQ), BF16)]
        + fields_held
        + [
            pltpu.VMEM((len(OFFSETS), 2 * rows + 16, MSG), BF16),
            pltpu.SemaphoreType.DMA((len(OFFSETS),)),
        ],
        compiler_params=pltpu.CompilerParams(vmem_limit_bytes=32 * MIB),
        cost_estimate=pl.CostEstimate(
            flops=2 * 2 * rows * slots * NQ * 3 * columns,
            bytes_accessed=20 * rows * columns,
            transcendentals=0,
        ),
        name="penalty",
    )(
        part_id,
        u_spec,
        dir_spec,
        table_row,
        table_col,
        degrees,
        degrees.T,
        jnp.asarray(edge_weight),
        jnp.asarray(mass_local),
        near,
    )

    d_back, u_returned[1] = lax.optimization_barrier((d_back, u_returned[1]))
    d_returned = [d_back[0]] + [None] * (modes - 1)
    for d in order:
        d_returned[d] = swap_with(d_back[d], "mode", d)
    advect, helm_velocity = finish(u_returned, range(modes), [None, local_u], mode_id)
    begun = finish(d_returned, [0], [local_d], mode_id)
    (helm_direction,) = finish(d_returned, range(1, modes), [local_d], mode_id, list(begun))
    return (advect, helm_velocity, helm_direction)


def solution(mesh):
    in_specs = (
        P("mode", "elem"),
        P("mode", "elem"),
        P(None, None, ("elem", "mode")),
        P(None, ("elem", "mode")),
        P(None, "elem"),
        P("elem"),
        P(None, "elem"),
    )
    out_specs = (P("mode", "elem"), P("mode", "elem"), P("mode", "elem"))
    return jax.shard_map(
        on_device, mesh=mesh, in_specs=in_specs, out_specs=out_specs, check_vma=False
    )
```
